512 devices in a mesh: tm: 32 (over z, x), row: 4 (over y_lo, core), col: 4 (over y_hi).
Axes of the slice: x: 4, y: 8 (y_hi: 4, y_lo: 2; y = y_hi * 2 + y_lo), z: 8, core: 2. Of those that a mesh axis runs over, the one named last changes fastest.
Arguments:
- query_tokens: bfloat16 [64, 32, 64, 1152], P('tm', 'row', 'col'), may hold values from -0.119628906 to 0.119628906
- key_tokens: bfloat16 [64, 32, 64, 1152], P('tm', 'row', 'col'), may hold values from -6 to 6
- value_tokens: bfloat16 [64, 32, 64, 1152], P('tm', 'row', 'col'), may hold values from -6 to 6
- grad_output: bfloat16 [64, 32, 64, 1152], P('tm', 'row', 'col'), may hold values from -6 to 6
- frame_decay: float32 [64, 36], P('tm'), may hold values from 0 to 1
- conv_weight: float32 [9, 1152], replicated, may hold values from -1.5 to 1.5
Outputs:
- query_grad: bfloat16 [64, 32, 64, 1152], P('tm', 'row', 'col')
- lookup_vector_gradient: bfloat16 [64, 32, 64, 1152], P('tm', 'row', 'col')
- value_grad: bfloat16 [64, 32, 64, 1152], P('tm', 'row', 'col')
The draws below stay inside these ranges and needn't reach their ends.
All inputs are finite; a program needn't handle non-finite values.
Results may differ from the reference program's by a relative error of at most 0.015.
Values may be sent and summed in bfloat16 or wider, within the bound.
No kernel may reach another device: no remote copies, remote signals or barrier semaphores. Data moves between devices by JAX's collectives and lax.ppermute only.
A program may use at most 64 MiB of HBM per device.

```python
import jax
import jax.numpy as jnp
from jax import lax

MIXING_CHANNELS = 36
HEAD_DIM = 32
CH = 1152
HIDDEN_SNAPSHOTS = 64
LROWS = 32
LCOLS = 64


def draw_frame_decay(key, part):
    key = jax.random.fold_in(key, 11)
    gathered_lookup_vectors = jax.random.split(key, 6)
    slow_share = 0.5
    slow_heads = jax.random.uniform(gathered_lookup_vectors[0], (MIXING_CHANNELS,)) < slow_share
    strength = jax.random.uniform(gathered_lookup_vectors[1], (MIXING_CHANNELS,), minval=0.2, maxval=1.0)
    jitter = jax.random.uniform(gathered_lookup_vectors[2], (HIDDEN_SNAPSHOTS, MIXING_CHANNELS), minval=0.5, maxval=2.0)
    slow_log = -strength[None, :] * jitter / HIDDEN_SNAPSHOTS
    fast_log = -jax.random.uniform(gathered_lookup_vectors[3], (HIDDEN_SNAPSHOTS, MIXING_CHANNELS), minval=0.6, maxval=1.6)
    natural_logarithm_decay = jnp.where(slow_heads[None, :], slow_log, fast_log)
    snapshot_clusters = jax.random.uniform(gathered_lookup_vectors[4], (HIDDEN_SNAPSHOTS, MIXING_CHANNELS)) < 3.0 / HIDDEN_SNAPSHOTS
    cluster_decay_factor = jax.random.uniform(gathered_lookup_vectors[5], (HIDDEN_SNAPSHOTS, MIXING_CHANNELS), minval=0.5, maxval=0.8)
    natural_logarithm_decay = natural_logarithm_decay + jnp.where(snapshot_clusters, jnp.log(cluster_decay_factor), 0.0)
    return jnp.exp(natural_logarithm_decay).astype(jnp.float32)


def shard_levels(rng, extent, pieces, low, top_value):
    level = 1.0
    for position, shards_of in pieces:
        draws = jax.random.uniform(jax.random.fold_in(jax.random.fold_in(rng, 6), position), (shards_of,), jnp.float32, low / len(pieces), top_value / len(pieces))
        level = level * jnp.repeat(jnp.exp(draws), extent[position] // shards_of).reshape((-1,) + (1,) * (len(extent) - 1 - position))
    return level


def gaussian(key, extent, scale, bound, cuts=(), dtype=jnp.bfloat16):
    level = shard_levels(key, extent, cuts, -0.22, 0.18) if cuts else 1.0
    values = jax.random.normal(key, extent, jnp.float32) * scale * level
    return jnp.minimum(jnp.maximum(values, -bound), bound).astype(dtype)


def setup_inputs(seed: int = 0) -> dict:
    streams_of = jax.random.split(jax.random.key(seed), 7)
    query_tokens = gaussian(streams_of[0], (HIDDEN_SNAPSHOTS, LROWS, LCOLS, CH), 0.02, 0.119628906, ((0, 32), (1, 4), (2, 4)))
    key_tokens = gaussian(streams_of[1], (HIDDEN_SNAPSHOTS, LROWS, LCOLS, CH), 1.0, 6.0, ((0, 32), (1, 4), (2, 4)))
    value_tokens = gaussian(streams_of[2], (HIDDEN_SNAPSHOTS, LROWS, LCOLS, CH), 1.0, 6.0, ((0, 32), (1, 4), (2, 4)))
    grad_output = gaussian(streams_of[3], (HIDDEN_SNAPSHOTS, LROWS, LCOLS, CH), 1.0, 6.0, ((0, 32), (1, 4), (2, 4)))
    frame_decay = draw_frame_decay(jax.random.fold_in(streams_of[6], 71), 0)
    conv_weight = gaussian(streams_of[5], (9, CH), 0.3, 1.5, (), jnp.float32)
    return dict(query_tokens=query_tokens, key_tokens=key_tokens, value_tokens=value_tokens, grad_output=grad_output, frame_decay=frame_decay, conv_weight=conv_weight)


def rectify(values):
    return jnp.maximum(values.astype(jnp.float32), 0.0)


def conv_back(grad_frame, conv_weight):
    padded = jnp.pad(grad_frame, ((1, 1), (1, 1), (0, 0)))
    result = grad_frame
    for row_off in (-1, 0, 1):
        for col_off in (-1, 0, 1):
            tap_index = (row_off + 1) * 3 + col_off + 1
            window = padded[1 - row_off:1 - row_off + LROWS, 1 - col_off:1 - col_off + LCOLS]
            result = result + conv_weight[tap_index] * window
    return result


def reference(query_tokens, key_tokens, value_tokens, grad_output, frame_decay, conv_weight):
    count = LROWS * LCOLS

    def split_heads(values):
        return values.reshape(HIDDEN_SNAPSHOTS, count, MIXING_CHANNELS, HEAD_DIM)

    queries = split_heads(query_tokens)
    keys_all = split_heads(key_tokens)
    values_all = split_heads(value_tokens)

    def frame_terms(inputs):
        keys_frame, vals_frame = inputs
        pos_keys = rectify(keys_frame)
        update = jnp.einsum("phd,phe->hde", pos_keys, vals_frame.astype(jnp.float32))
        return update, jnp.sum(pos_keys, axis=0)

    state_updates, normalizer_summands = lax.map(frame_terms, (keys_all, values_all))

    def forward_step(carry, inputs):
        state, normal = carry
        decay_row, update, zterm = inputs
        state = decay_row[:, None, None] * state + update
        normal = decay_row[:, None] * normal + zterm
        return (state, normal), (state, normal)

    start = (jnp.zeros((MIXING_CHANNELS, HEAD_DIM, HEAD_DIM), jnp.float32), jnp.zeros((MIXING_CHANNELS, HEAD_DIM), jnp.float32))
    _, (states, normals) = lax.scan(forward_step, start, (frame_decay, state_updates, normalizer_summands))

    def frame_backward(inputs):
        query_frame, state, normal, grad_frame = inputs
        pos_q = rectify(query_frame)
        numer = jnp.einsum("phd,hde->phe", pos_q, state)
        denom = jnp.einsum("phd,hd->ph", pos_q, normal) + 1.0
        attn = numer / denom[..., None]
        grad_attn = conv_back(grad_frame.astype(jnp.float32), conv_weight).reshape(count, MIXING_CHANNELS, HEAD_DIM)
        grad_num = grad_attn / denom[..., None]
        grad_den = -jnp.sum(grad_attn * attn, axis=-1) / denom
        grad_posq = jnp.einsum("phe,hde->phd", grad_num, state) + grad_den[..., None] * normal[None]
        query_grad = jnp.where(query_frame > 0, grad_posq, 0.0).astype(jnp.bfloat16)
        local = jnp.einsum("phd,phe->hde", pos_q, grad_num)
        localz = jnp.einsum("ph,phd->hd", grad_den, pos_q)
        return query_grad, local, localz

    query_grad, locals_all, localz_all = lax.map(frame_backward, (queries, states, normals, grad_output))

    def reverse_step(carry, inputs):
        carry_state, carry_normal = carry
        decay_row, local, localz = inputs
        total = local + carry_state
        totalz = localz + carry_normal
        return (decay_row[:, None, None] * total, decay_row[:, None] * totalz), (total, totalz)

    _, (carried, carriedz) = lax.scan(reverse_step, start, (frame_decay, locals_all, localz_all), reverse=True)

    def frame_keys(inputs):
        keys_frame, vals_frame, total, totalz = inputs
        pos_keys = rectify(keys_frame)
        grad_posk = jnp.einsum("phe,hde->phd", vals_frame.astype(jnp.float32), total) + totalz[None]
        lookup_vector_gradient = jnp.where(keys_frame > 0, grad_posk, 0.0).astype(jnp.bfloat16)
        value_grad = jnp.einsum("phd,hde->phe", pos_keys, total).astype(jnp.bfloat16)
        return lookup_vector_gradient, value_grad

    lookup_vector_gradient, value_grad = lax.map(frame_keys, (keys_all, values_all, carried, carriedz))
    shape = (HIDDEN_SNAPSHOTS, LROWS, LCOLS, CH)
    return query_grad.reshape(shape), lookup_vector_gradient.reshape(shape), value_grad.reshape(shape)
```

```python
import jax
import jax.numpy as jnp
from jax import lax
from jax.experimental import pallas as pl
from jax.experimental.pallas import tpu as pltpu
from jax.sharding import PartitionSpec as P

HEADS = 36
DIM = 32
LANES = 128
GROUPS = HEADS * DIM // LANES
PER_GROUP = LANES // DIM
FRAMES = 2
ROWS = 8
COLS = 16
TOKENS = ROWS * COLS
CH = HEADS * DIM
OWNERS = 16
HALF = DIM // 2
NORMAL = 2 * GROUPS
EXTRA = NORMAL + 1
SLOTS = 20
OWNED = FRAMES * SLOTS
SPACE = ("row", "col")
VMEM_BYTES = 24 * 1024 * 1024
F32 = jnp.float32
BF16 = jnp.bfloat16


def call(body, outs, *args, scratch=(), flops=1_000_000, name=None):
    out_shape = tuple(jax.ShapeDtypeStruct(shape, dtype) for shape, dtype in outs)
    moved = sum(a.size * a.dtype.itemsize for a in args) + sum(o.size * o.dtype.itemsize for o in out_shape)
    return pl.pallas_call(
        body,
        out_shape=out_shape,
        in_specs=[pl.BlockSpec(memory_space=pltpu.VMEM)] * len(args),
        out_specs=tuple(pl.BlockSpec(memory_space=pltpu.VMEM) for _ in outs),
        scratch_shapes=list(scratch),
        compiler_params=pltpu.CompilerParams(vmem_limit_bytes=VMEM_BYTES),
        cost_estimate=pl.CostEstimate(flops=flops, bytes_accessed=moved, transcendentals=0),
        name=name,
    )(*args)


def dot(a, b, contract=((1,), (0,)), precision=None):
    return lax.dot_general(a, b, (contract, ((), ())), preferred_element_type=F32, precision=precision)


def iota(shape, dim):
    return lax.broadcasted_iota(jnp.int32, shape, dim)


def lane_head(shape):
    return iota(shape, 1) // DIM


def compact(square):
    head = lane_head((DIM, LANES))
    out = square[(PER_GROUP - 1) * DIM :]
    for i in reversed(range(PER_GROUP - 1)):
        out = jnp.where(head == i, square[i * DIM : (i + 1) * DIM], out)
    return out


def spread(rows):
    head = lane_head((DIM, LANES))
    return jnp.concatenate([jnp.where(head == i, rows, 0.0) for i in range(PER_GROUP)], axis=0).astype(BF16)


def head_ones():
    return (iota((LANES, LANES), 0) // DIM == lane_head((LANES, LANES))).astype(BF16)


def clear_unused(held):
    for owner in range(OWNERS):
        for f in range(FRAMES):
            first = owner * OWNED + f * SLOTS + (EXTRA if owner < GROUPS else NORMAL)
            last = owner * OWNED + (f + 1) * SLOTS
            held[first:last, :] = jnp.zeros((last - first, LANES), F32)


def put_rows(held, f, g, rows, normal):
    for half in range(2):
        held[pl.ds(f * SLOTS + half * GROUPS + g, OWNERS, stride=OWNED), :] = rows[half * HALF : (half + 1) * HALF]
    at = g * OWNED + f * SLOTS + NORMAL
    held[at : at + 1, :] = normal


def take_rows(held, f, g):
    rows = jnp.concatenate(
        [held[pl.ds(f * SLOTS + half * GROUPS + g, OWNERS, stride=OWNED), :] for half in range(2)], axis=0
    )
    at = g * OWNED + f * SLOTS + NORMAL
    return rows, held[at : at + 1, :]


def part(ref, f, g):
    return ref[f * TOKENS : (f + 1) * TOKENS, g * LANES : (g + 1) * LANES]


def update_kernel(k_ref, v_ref, out_ref, held):
    clear_unused(held)
    for f in range(FRAMES):
        for g in range(GROUPS):
            pos_k = jnp.maximum(part(k_ref, f, g), 0)
            rows = compact(dot(pos_k, part(v_ref, f, g), ((0,), (0,))))
            put_rows(held, f, g, rows, jnp.sum(pos_k.astype(F32), axis=0, keepdims=True))
    out_ref[...] = held[...].astype(BF16)


def decay_kernel(decay_ref, lanes_ref, row_ref):
    mine = lax.axis_index("row") * lax.axis_size("col") + lax.axis_index("col")
    decay = decay_ref[...]
    slot = iota((SLOTS, HEADS), 0)
    group = jnp.where(slot < GROUPS, slot, jnp.where(slot < NORMAL, slot - GROUPS, mine))
    own = iota((SLOTS, HEADS), 1) // PER_GROUP == group
    onto = (iota((HEADS, LANES), 0) % PER_GROUP == lane_head((HEADS, LANES))).astype(F32)
    for f in range(FRAMES):
        picked = jnp.where(own, decay[f : f + 1], 0.0)
        lanes_ref[f * SLOTS : (f + 1) * SLOTS, :] = dot(picked, onto, precision=lax.Precision.HIGHEST)
    rest = jnp.broadcast_to(decay[0:1] * decay[1:2], (8, HEADS))
    row = jnp.zeros((8, LANES), F32)
    for third in range(3):
        piece = rest.astype(BF16)
        rest = rest - piece.astype(F32)
        row = row + dot(piece, (iota((HEADS, LANES), 1) == iota((HEADS, LANES), 0) + third * HEADS).astype(BF16))
    row_ref[...] = row


def frame_sums(x_ref):
    return jnp.sum(x_ref[...].astype(F32).reshape(OWNERS, OWNED, LANES), axis=0)


def copies(block, out_ref):
    count = out_ref.shape[0] // block.shape[0]
    out_ref[...] = jnp.broadcast_to(block[None], (count,) + block.shape).reshape(out_ref.shape).astype(BF16)


def block_forward_kernel(x_ref, lanes_ref, row_ref, sums_ref, out_ref):
    sums = frame_sums(x_ref)
    sums_ref[...] = sums
    total = lanes_ref[SLOTS:, :] * sums[:SLOTS] + sums[SLOTS:]
    total = jnp.where(iota((SLOTS, LANES), 0) == EXTRA, row_ref[0:1, :], total)
    copies(jnp.concatenate([total, total], axis=0), out_ref)


def block_reverse_kernel(x_ref, lanes_ref, sums_ref, out_ref):
    sums = frame_sums(x_ref)
    sums_ref[...] = sums
    total = lanes_ref[:SLOTS, :] * (sums[:SLOTS] + lanes_ref[SLOTS:, :] * sums[SLOTS:])
    copies(jnp.concatenate([total, total], axis=0), out_ref)


def shifted(x, by, count):
    row = iota(x.shape, 0)
    if by > 0:
        return jnp.where(row < by, 1.0, pltpu.roll(x, by, 0))
    return jnp.where(row >= count + by, 1.0, pltpu.roll(x, count + by, 0))


def block_weights(held, index, count, backward):
    mine = lax.axis_index("tm")
    decays = held[pl.ds(EXTRA, count, stride=SLOTS), :].astype(BF16)
    source = iota((LANES, LANES), 0)
    onto = (source < 3 * HEADS) & (source % HEADS == index * PER_GROUP + lane_head((LANES, LANES)))
    block = dot(decays, onto.astype(BF16))
    at = iota((count, LANES), 0)
    between = at > mine if backward else at < mine
    product = shifted(jnp.where(between, block, 1.0), 1 if backward else -1, count)
    step = 1
    while step < count:
        product = product * shifted(product, step if backward else -step, count)
        step *= 2
    return jnp.where(between, product, 0.0)


def weights_kernel(y_ref, out_ref, held):
    count = y_ref.shape[0] // SLOTS
    held[...] = y_ref[...].astype(F32)
    mine = lax.axis_index("row") * lax.axis_size("col") + lax.axis_index("col")
    for i in range(GROUPS + 1):
        out_ref[i] = block_weights(held, i if i < GROUPS else mine, count, True)


def entering(held, carry, weights, count):
    carry[...] = jnp.zeros(carry.shape, F32)
    for slot in range(NORMAL + 1):
        weight = weights[GROUPS if slot == NORMAL else slot % GROUPS]
        rows = held[pl.ds(slot, count, stride=SLOTS), :]
        carry[slot : slot + 1, :] = jnp.sum(weight * rows, axis=0, keepdims=True)
    return carry[:SLOTS, :]


def states_kernel(y_ref, sums_ref, lanes_ref, out_ref, held, carry):
    count = y_ref.shape[0] // SLOTS
    held[...] = y_ref[...].astype(F32)
    mine = lax.axis_index("row") * lax.axis_size("col") + lax.axis_index("col")
    weights = [block_weights(held, i if i < GROUPS else mine, count, False) for i in range(GROUPS + 1)]
    before = entering(held, carry, weights, count)
    first = lanes_ref[:SLOTS, :] * before + sums_ref[:SLOTS, :]
    second = lanes_ref[SLOTS:, :] * first + sums_ref[SLOTS:, :]
    copies(jnp.concatenate([first, second], axis=0), out_ref)


def carried_kernel(y_ref, sums_ref, lanes_ref, weights_ref, out_ref, held, carry):
    count = y_ref.shape[0] // SLOTS
    held[...] = y_ref[...].astype(F32)
    after = entering(held, carry, [weights_ref[i] for i in range(GROUPS + 1)], count)
    second = sums_ref[SLOTS:, :] + after
    first = sums_ref[:SLOTS, :] + lanes_ref[SLOTS:, :] * second
    copies(jnp.concatenate([first, second], axis=0), out_ref)


def conv_kernel(g_ref, above_ref, below_ref, left_ref, right_ref, weight_ref, out_ref):
    at = iota((COLS, LANES), 0)
    for f in range(FRAMES):
        left = left_ref[f].astype(F32)
        right = right_ref[f].astype(F32)
        for g in range(GROUPS):
            lanes = slice(g * LANES, (g + 1) * LANES)
            taps = [weight_ref[t : t + 1, lanes] for t in range(9)]
            total = [None] * ROWS
            for source in range(-1, ROWS + 1):
                if source < 0:
                    x = above_ref[f, :, lanes]
                elif source == ROWS:
                    x = below_ref[f, :, lanes]
                else:
                    first = (f * ROWS + source) * COLS
                    x = g_ref[first : first + COLS, lanes]
                x = x.astype(F32)
                from_left = jnp.where(at == 0, left[source + 1 : source + 2, lanes], pltpu.roll(x, 1, 0))
                from_right = jnp.where(
                    at == COLS - 1, right[source + 1 : source + 2, lanes], pltpu.roll(x, COLS - 1, 0)
                )
                for row_off in (-1, 0, 1):
                    row = source + row_off
                    if 0 <= row < ROWS:
                        tap = (row_off + 1) * 3
                        add = taps[tap] * from_right + taps[tap + 1] * x + taps[tap + 2] * from_left
                        if row_off == 0:
                            add = add + x
                        total[row] = add if total[row] is None else total[row] + add
            for row in range(ROWS):
                first = (f * ROWS + row) * COLS
                out_ref[first : first + COLS, lanes] = total[row]


def query_kernel(q_ref, ga_ref, z_ref, grad_ref, out_ref, held, sent):
    held[...] = z_ref[...].astype(F32)
    clear_unused(sent)
    ones = head_ones()
    for f in range(FRAMES):
        for g in range(GROUPS):
            rows, normal = take_rows(held, f, g)
            state = spread(rows)
            query = part(q_ref, f, g)
            pos_q = jnp.maximum(query, 0)
            pos_qf = pos_q.astype(F32)
            grad_attn = part(ga_ref, f, g)
            inverse = 1.0 / (dot((pos_qf * normal).astype(BF16), ones) + 1.0)
            attn = dot(pos_q, state) * inverse
            grad_num = grad_attn * inverse
            grad_den = -dot((grad_attn * attn).astype(BF16), ones) * inverse
            grad_num = grad_num.astype(BF16)
            grad_posq = dot(grad_num, state, ((1,), (1,))) + grad_den * normal
            grad_ref[f * TOKENS : (f + 1) * TOKENS, g * LANES : (g + 1) * LANES] = jnp.where(
                pos_qf > 0, grad_posq, 0.0
            ).astype(BF16)
            local = compact(dot(pos_q, grad_num, ((0,), (0,))))
            put_rows(sent, f, g, local, jnp.sum(grad_den * pos_qf, axis=0, keepdims=True))
    out_ref[...] = sent[...].astype(BF16)


def key_kernel(k_ref, v_ref, z_ref, key_grad_ref, value_grad_ref, held):
    held[...] = z_ref[...].astype(F32)
    for f in range(FRAMES):
        for g in range(GROUPS):
            rows, normal = take_rows(held, f, g)
            carried = spread(rows)
            keys = part(k_ref, f, g)
            here = (slice(f * TOKENS, (f + 1) * TOKENS), slice(g * LANES, (g + 1) * LANES))
            grad = dot(part(v_ref, f, g), carried, ((1,), (1,))) + normal
            key_grad_ref[here] = jnp.where(keys.astype(F32) > 0, grad, 0.0).astype(BF16)
            value_grad_ref[here] = dot(jnp.maximum(keys, 0), carried).astype(BF16)


def exchange(block, axes, count):
    rows = block.shape[0] // count
    block = block.reshape(count, rows // 2, 2, LANES)
    return lax.all_to_all(block, axes, 0, 0, tiled=True).reshape(count * rows, LANES)


def neighbours(cells, axis, dim):
    count, size = lax.axis_size(axis), cells.shape[dim]
    tail = lax.slice_in_dim(cells, size - 1, size, axis=dim)
    head = lax.slice_in_dim(cells, 0, 1, axis=dim)
    up = lax.ppermute(tail, axis, [(i, i + 1) for i in range(count - 1)])
    down = lax.ppermute(head, axis, [(i + 1, i) for i in range(count - 1)])
    return up, down


def per_device(query_tokens, key_tokens, value_tokens, grad_output, frame_decay, conv_weight):
    shape = query_tokens.shape
    flat = (FRAMES * TOKENS, CH)
    blocks = lax.axis_size("tm")
    q, k, v, g = (x.reshape(flat) for x in (query_tokens, key_tokens, value_tokens, grad_output))
    space = ((OWNERS * OWNED, LANES), BF16)
    time = ((blocks * SLOTS, LANES), BF16)
    owned = ((OWNED, LANES), F32)
    held_space = pltpu.VMEM(space[0], F32)
    held_time = pltpu.VMEM(time[0], F32)
    carry = pltpu.VMEM((24, LANES), F32)
    work = 2 * FRAMES * GROUPS * TOKENS * LANES * LANES

    above, below = neighbours(grad_output, "row", 1)
    (sent,) = call(update_kernel, [space], k, v, scratch=[held_space], flops=work, name="update")
    lanes, decay_row = call(decay_kernel, [owned, ((8, LANES), F32)], frame_decay, name="decay")
    tall = jnp.concatenate([above, grad_output, below], axis=1)
    left, right = neighbours(tall, "col", 2)

    x = exchange(sent, SPACE, OWNERS)
    sums, sent = call(block_forward_kernel, [owned, time], x, lanes, decay_row, name="block_forward")
    y = exchange(sent, "tm", blocks)
    (sent,) = call(states_kernel, [space], y, sums, lanes, scratch=[held_time, carry], name="states")
    (weights,) = call(
        weights_kernel, [((GROUPS + 1, blocks, LANES), F32)], y, scratch=[held_time], name="reverse_weights"
    )
    z = exchange(sent, SPACE, OWNERS)
    (grad_attn,) = call(
        conv_kernel,
        [(flat, F32)],
        g,
        above.reshape(FRAMES, COLS, CH),
        below.reshape(FRAMES, COLS, CH),
        left.reshape(FRAMES, ROWS + 2, CH),
        right.reshape(FRAMES, ROWS + 2, CH),
        conv_weight,
        flops=20 * flat[0] * flat[1],
        name="conv",
    )
    query_grad, sent = call(
        query_kernel, [(flat, BF16), space], q, grad_attn, z, scratch=[held_space, held_space], flops=5 * work, name="query"
    )
    x = exchange(sent, SPACE, OWNERS)
    sums, sent = call(block_reverse_kernel, [owned, time], x, lanes, name="block_reverse")
    y = exchange(sent, "tm", blocks)
    (sent,) = call(carried_kernel, [space], y, sums, lanes, weights, scratch=[held_time, carry], name="carried")
    z = exchange(sent, SPACE, OWNERS)
    key_grad, value_grad = call(
        key_kernel, [(flat, BF16), (flat, BF16)], k, v, z, scratch=[held_space], flops=2 * work, name="key"
    )
    return query_grad.reshape(shape), key_grad.reshape(shape), value_grad.reshape(shape)


def solution(mesh):
    tokens = P("tm", "row", "col", None)
    return jax.shard_map(
        per_device,
        mesh=mesh,
        in_specs=(tokens, tokens, tokens, tokens, P("tm", None), P()),
        out_specs=(tokens, tokens, tokens),
        check_vma=False,
    )
```

```python
import jax
import jax.numpy as jnp
from jax import lax
from jax.experimental import pallas as pl
from jax.experimental.pallas import tpu as pltpu
from jax.sharding import PartitionSpec as P

HEADS = 36
DIM = 32
LANES = 128
GROUPS = HEADS * DIM // LANES
PER_GROUP = LANES // DIM
FRAMES = 2
ROWS = 8
COLS = 16
TOKENS = ROWS * COLS
CH = HEADS * DIM
OWNERS = 16
HALF = DIM // 2
STATES = 2 * GROUPS
EXTRA = STATES + GROUPS
SLOTS = EXTRA + 1
OWNED = FRAMES * SLOTS
BOTH = 2 * FRAMES * STATES
SPACE = ("row", "col")
VMEM_BYTES = 16 * 1024 * 1024
F32 = jnp.float32
BF16 = jnp.bfloat16


def call(body, outs, *args, scratch=(), flops=1_000_000, unread=0, name=None):
    out_shape = tuple(jax.ShapeDtypeStruct(shape, dtype) for shape, dtype in outs)
    moved = sum(a.size * a.dtype.itemsize for a in args) + sum(o.size * o.dtype.itemsize for o in out_shape)
    return pl.pallas_call(
        body,
        out_shape=out_shape,
        in_specs=[pl.BlockSpec(memory_space=pltpu.VMEM)] * (len(args) - unread)
        + [pl.BlockSpec(memory_space=pl.ANY)] * unread,
        out_specs=tuple(pl.BlockSpec(memory_space=pltpu.VMEM) for _ in outs),
        scratch_shapes=list(scratch),
        compiler_params=pltpu.CompilerParams(vmem_limit_bytes=VMEM_BYTES),
        cost_estimate=pl.CostEstimate(flops=flops, bytes_accessed=moved, transcendentals=0),
        name=name,
    )(*args)


def dot(a, b, contract=((1,), (0,)), precision=None):
    return lax.dot_general(a, b, (contract, ((), ())), preferred_element_type=F32, precision=precision)


def iota(shape, dim):
    return lax.broadcasted_iota(jnp.int32, shape, dim)


def lane_head(shape):
    return iota(shape, 1) // DIM


def compact(square):
    head = lane_head((DIM, LANES))
    out = square[(PER_GROUP - 1) * DIM :]
    for i in reversed(range(PER_GROUP - 1)):
        out = jnp.where(head == i, square[i * DIM : (i + 1) * DIM], out)
    return out


def spread(rows):
    head = lane_head((DIM, LANES))
    return jnp.concatenate([jnp.where(head == i, rows, 0.0) for i in range(PER_GROUP)], axis=0).astype(BF16)


def head_ones():
    return (iota((LANES, LANES), 0) // DIM == lane_head((LANES, LANES))).astype(BF16)


def put_rows(held, size, start, rows):
    for half in range(2):
        held[pl.ds(start + half * GROUPS, OWNERS, stride=size), :] = rows[half * HALF : (half + 1) * HALF]


def take_rows(held, size, start):
    return jnp.concatenate([held[pl.ds(start + half * GROUPS, OWNERS, stride=size), :] for half in range(2)], axis=0)


def part(ref, f, g):
    return ref[f * TOKENS : (f + 1) * TOKENS, g * LANES : (g + 1) * LANES]


def update_kernel(k_ref, v_ref, out_ref, held):
    for f in range(FRAMES):
        held[pl.ds(f * SLOTS + EXTRA, OWNERS, stride=OWNED), :] = jnp.zeros((OWNERS, LANES), F32)
        for g in range(GROUPS):
            pos_k = jnp.maximum(part(k_ref, f, g), 0)
            put_rows(held, OWNED, f * SLOTS + g, compact(dot(pos_k, part(v_ref, f, g), ((0,), (0,)))))
            normal = jnp.sum(pos_k.astype(F32), axis=0, keepdims=True)
            held[pl.ds(f * SLOTS + STATES + g, OWNERS, stride=OWNED), :] = jnp.broadcast_to(normal, (OWNERS, LANES))
    out_ref[...] = held[...].astype(BF16)


def decay_kernel(decay_ref, lanes_ref, row_ref):
    decay = decay_ref[...]
    own = iota((SLOTS, HEADS), 1) // PER_GROUP == iota((SLOTS, HEADS), 0) % GROUPS
    onto = (iota((HEADS, LANES), 0) % PER_GROUP == lane_head((HEADS, LANES))).astype(F32)
    for f in range(FRAMES):
        picked = jnp.where(own, decay[f : f + 1], 0.0)
        lanes_ref[f * SLOTS : (f + 1) * SLOTS, :] = dot(picked, onto, precision=lax.Precision.HIGHEST)
    rest = jnp.broadcast_to(decay[0:1] * decay[1:2], (8, HEADS))
    row = jnp.zeros((8, LANES), F32)
    for third in range(3):
        piece = rest.astype(BF16)
        rest = rest - piece.astype(F32)
        row = row + dot(piece, (iota((HEADS, LANES), 1) == iota((HEADS, LANES), 0) + third * HEADS).astype(BF16))
    row_ref[...] = row


def frame_sums(x_ref):
    return jnp.sum(x_ref[...].astype(F32).reshape(OWNERS, OWNED, LANES), axis=0)


def copies(block, out_ref):
    count = out_ref.shape[0] // block.shape[0]
    out_ref[...] = jnp.broadcast_to(block[None], (count,) + block.shape).reshape(out_ref.shape).astype(BF16)


def block_forward_kernel(x_ref, lanes_ref, row_ref, above_ref, below_ref, sums_ref, out_ref):
    del above_ref, below_ref
    sums = frame_sums(x_ref)
    sums_ref[...] = sums
    total = lanes_ref[SLOTS:, :] * sums[:SLOTS] + sums[SLOTS:]
    total = jnp.where(iota((SLOTS, LANES), 0) == EXTRA, row_ref[0:1, :], total)
    copies(jnp.concatenate([total, total], axis=0), out_ref)


def shifted(x, by, count):
    row = iota(x.shape, 0)
    if by > 0:
        return jnp.where(row < by, 1.0, pltpu.roll(x, by, 0))
    return jnp.where(row >= count + by, 1.0, pltpu.roll(x, count + by, 0))


def block_weights(held, index, count, backward):
    mine = lax.axis_index("tm")
    decays = held[pl.ds(EXTRA, count, stride=SLOTS), :].astype(BF16)
    source = iota((LANES, LANES), 0)
    onto = (source < 3 * HEADS) & (source % HEADS == index * PER_GROUP + lane_head((LANES, LANES)))
    block = dot(decays, onto.astype(BF16))
    at = iota((count, LANES), 0)
    between = at > mine if backward else at < mine
    product = shifted(jnp.where(between, block, 1.0), 1 if backward else -1, count)
    step = 1
    while step < count:
        product = product * shifted(product, step if backward else -step, count)
        step *= 2
    return jnp.where(between, product, 0.0)


def entering(held, carry, weights, count):
    carry[EXTRA:SLOTS, :] = jnp.zeros((1, LANES), F32)
    for slot in range(EXTRA):
        rows = held[pl.ds(slot, count, stride=SLOTS), :]
        carry[slot : slot + 1, :] = jnp.sum(weights[slot % GROUPS] * rows, axis=0, keepdims=True)
    return carry[:SLOTS, :]


def states_kernel(y_ref, sums_ref, lanes_ref, q_ref, ga_ref, own_ref, inverse_ref, num_ref, out_ref, after_ref, held, carry, sent):
    count = y_ref.shape[0] // SLOTS
    held[...] = y_ref[...].astype(F32)
    weights = [block_weights(held, g, count, False) for g in range(GROUPS)]
    before = entering(held, carry, weights, count)
    for g in range(GROUPS):
        after_ref[g] = block_weights(held, g, count, True)
    first = lanes_ref[:SLOTS, :] * before + sums_ref[:SLOTS, :]
    second = lanes_ref[SLOTS:, :] * first + sums_ref[SLOTS:, :]
    own_ref[:SLOTS, :] = first
    own_ref[SLOTS:, :] = second
    for owner in range(OWNERS):
        sent[owner * BOTH : owner * BOTH + STATES, :] = first[:STATES]
        sent[owner * BOTH + STATES : owner * BOTH + 2 * STATES, :] = second[:STATES]
    ones = head_ones()
    for f in range(FRAMES):
        for g in range(GROUPS):
            normal = (first, second)[f][STATES + g : STATES + g + 1]
            pos_q = jnp.maximum(part(q_ref, f, g), 0)
            inverse = 1.0 / (dot((pos_q.astype(F32) * normal).astype(BF16), ones) + 1.0)
            grad_num = (part(ga_ref, f, g) * inverse).astype(BF16)
            here = (slice(f * TOKENS, (f + 1) * TOKENS), slice(g * LANES, (g + 1) * LANES))
            inverse_ref[here] = inverse
            num_ref[here] = grad_num
            put_rows(sent, BOTH, (FRAMES + f) * STATES + g, compact(dot(pos_q, grad_num, ((0,), (0,)))))
    out_ref[...] = sent[...].astype(BF16)


def locals_kernel(z_ref, q_ref, num_ref, inverse_ref, lanes_ref, sums_ref, den_ref, out_ref, held):
    held[...] = z_ref[...].astype(F32)
    sums = jnp.sum(z_ref[...].astype(F32).reshape(OWNERS, BOTH, LANES), axis=0)
    ones = head_ones()
    lane = iota((TOKENS, LANES), 1) % DIM
    for f in range(FRAMES):
        sums_ref[f * SLOTS : f * SLOTS + STATES, :] = sums[(FRAMES + f) * STATES : (FRAMES + f + 1) * STATES]
        sums_ref[f * SLOTS + EXTRA : (f + 1) * SLOTS, :] = jnp.zeros((1, LANES), F32)
        packed = jnp.zeros((TOKENS, LANES), F32)
        for g in range(GROUPS):
            state = spread(take_rows(held, BOTH, f * STATES + g))
            pos_q = jnp.maximum(part(q_ref, f, g), 0)
            product = part(num_ref, f, g).astype(F32) * dot(pos_q, state)
            grad_den = -dot(product.astype(BF16), ones) * part(inverse_ref, f, g)
            packed = packed + jnp.where(lane == g, grad_den, 0.0)
            at = f * SLOTS + STATES + g
            sums_ref[at : at + 1, :] = jnp.sum(grad_den * pos_q.astype(F32), axis=0, keepdims=True)
        den_ref[f * TOKENS : (f + 1) * TOKENS, :] = packed.astype(BF16)
    total = lanes_ref[:SLOTS, :] * (sums_ref[:SLOTS, :] + lanes_ref[SLOTS:, :] * sums_ref[SLOTS:, :])
    copies(jnp.concatenate([total, total], axis=0), out_ref)


def query_kernel(z_ref, q_ref, num_ref, den_ref, own_ref, grad_ref, held):
    held[...] = z_ref[...].astype(F32)
    source = iota((LANES, LANES), 0)
    same = source // DIM == lane_head((LANES, LANES))
    for f in range(FRAMES):
        den = den_ref[f * TOKENS : (f + 1) * TOKENS, :]
        for g in range(GROUPS):
            state = spread(take_rows(held, BOTH, f * STATES + g))
            at = f * SLOTS + STATES + g
            here = (slice(f * TOKENS, (f + 1) * TOKENS), slice(g * LANES, (g + 1) * LANES))
            grad_den = dot(den, (same & (source % DIM == g)).astype(BF16))
            grad = dot(num_ref[here], state, ((1,), (1,))) + grad_den * own_ref[at : at + 1, :]
            grad_ref[here] = jnp.where(q_ref[here].astype(F32) > 0, grad, 0.0).astype(BF16)


def carried_kernel(y_ref, sums_ref, lanes_ref, weights_ref, query_ref, out_ref, held, carry):
    del query_ref
    count = y_ref.shape[0] // SLOTS
    held[...] = y_ref[...].astype(F32)
    after = entering(held, carry, [weights_ref[g] for g in range(GROUPS)], count)
    second = sums_ref[SLOTS:, :] + after
    first = sums_ref[:SLOTS, :] + lanes_ref[SLOTS:, :] * second
    copies(jnp.concatenate([first, second], axis=0), out_ref)


def conv_kernel(g_ref, above_ref, below_ref, left_ref, right_ref, weight_ref, out_ref):
    at = iota((COLS, LANES), 0)
    for f in range(FRAMES):
        left = left_ref[f].astype(F32)
        right = right_ref[f].astype(F32)
        for g in range(GROUPS):
            lanes = slice(g * LANES, (g + 1) * LANES)
            taps = [weight_ref[t : t + 1, lanes] for t in range(9)]
            total = [None] * ROWS
            for source in range(-1, ROWS + 1):
                if source < 0:
                    x = above_ref[f, :, lanes]
                elif source == ROWS:
                    x = below_ref[f, :, lanes]
                else:
                    first = (f * ROWS + source) * COLS
                    x = g_ref[first : first + COLS, lanes]
                x = x.astype(F32)
                from_left = jnp.where(at == 0, left[source + 1 : source + 2, lanes], pltpu.roll(x, 1, 0))
                from_right = jnp.where(
                    at == COLS - 1, right[source + 1 : source + 2, lanes], pltpu.roll(x, COLS - 1, 0)
                )
                for row_off in (-1, 0, 1):
                    row = source + row_off
                    if 0 <= row < ROWS:
                        tap = (row_off + 1) * 3
                        add = taps[tap] * from_right + taps[tap + 1] * x + taps[tap + 2] * from_left
                        if row_off == 0:
                            add = add + x
                        total[row] = add if total[row] is None else total[row] + add
            for row in range(ROWS):
                first = (f * ROWS + row) * COLS
                out_ref[first : first + COLS, lanes] = total[row]


def key_kernel(k_ref, v_ref, z_ref, key_grad_ref, value_grad_ref, held):
    held[...] = z_ref[...].astype(F32)
    sums = frame_sums(z_ref)
    for f in range(FRAMES):
        for g in range(GROUPS):
            carried = spread(take_rows(held, OWNED, f * SLOTS + g))
            at = f * SLOTS + STATES + g
            keys = part(k_ref, f, g)
            here = (slice(f * TOKENS, (f + 1) * TOKENS), slice(g * LANES, (g + 1) * LANES))
            grad = dot(part(v_ref, f, g), carried, ((1,), (1,))) + sums[at : at + 1]
            key_grad_ref[here] = jnp.where(keys.astype(F32) > 0, grad, 0.0).astype(BF16)
            value_grad_ref[here] = dot(jnp.maximum(keys, 0), carried).astype(BF16)


def exchange(block, axes, count):
    rows = block.shape[0] // count
    block = block.reshape(count, rows // 2, 2, LANES)
    return lax.all_to_all(block, axes, 0, 0, tiled=True).reshape(count * rows, LANES)


def neighbours(cells, axis, dim):
    count, size = lax.axis_size(axis), cells.shape[dim]
    tail = lax.slice_in_dim(cells, size - 1, size, axis=dim)
    head = lax.slice_in_dim(cells, 0, 1, axis=dim)
    up = lax.ppermute(tail, axis, [(i, i + 1) for i in range(count - 1)])
    down = lax.ppermute(head, axis, [(i + 1, i) for i in range(count - 1)])
    return up, down


def per_device(query_tokens, key_tokens, value_tokens, grad_output, frame_decay, conv_weight):
    shape = query_tokens.shape
    flat = (FRAMES * TOKENS, CH)
    blocks = lax.axis_size("tm")
    q, k, v, g = (x.reshape(flat) for x in (query_tokens, key_tokens, value_tokens, grad_output))
    space = ((OWNERS * OWNED, LANES), BF16)
    both = ((OWNERS * BOTH, LANES), BF16)
    time = ((blocks * SLOTS, LANES), BF16)
    owned = ((OWNED, LANES), F32)
    held_space, held_both, held_time = (pltpu.VMEM(kind[0], F32) for kind in (space, both, time))
    carry = pltpu.VMEM((32, LANES), F32)
    work = 2 * FRAMES * GROUPS * TOKENS * LANES * LANES

    above, below = neighbours(grad_output, "row", 1)
    (sent,) = call(update_kernel, [space], k, v, scratch=[held_space], flops=work, name="update")
    lanes, decay_row = call(decay_kernel, [owned, ((8, LANES), F32)], frame_decay, name="decay")
    x = exchange(sent, SPACE, OWNERS)
    tall = jnp.concatenate([above, grad_output, below], axis=1)
    left, right = neighbours(tall, "col", 2)
    above, below = (edge.reshape(FRAMES, COLS, CH) for edge in (above, below))
    left, right = (edge.reshape(FRAMES, ROWS + 2, CH) for edge in (left, right))
    sums, sent = call(
        block_forward_kernel, [owned, time], x, lanes, decay_row, above, below, unread=2, name="block_forward"
    )
    y = exchange(sent, "tm", blocks)
    (grad_attn,) = call(
        conv_kernel, [(flat, F32)], g, above, below, left, right, conv_weight, flops=20 * flat[0] * flat[1], name="conv"
    )
    own, inverse, grad_num, sent, weights = call(
        states_kernel,
        [owned, (flat, F32), (flat, BF16), both, ((GROUPS, blocks, LANES), F32)],
        y,
        sums,
        lanes,
        q,
        grad_attn,
        scratch=[held_time, carry, held_both],
        flops=2 * work,
        name="states",
    )
    z = exchange(sent, SPACE, OWNERS)
    sums, grad_den, sent = call(
        locals_kernel,
        [owned, ((FRAMES * TOKENS, LANES), BF16), time],
        z,
        q,
        grad_num,
        inverse,
        lanes,
        scratch=[held_both],
        flops=2 * work,
        name="locals",
    )
    y = exchange(sent, "tm", blocks)
    (query_grad,) = call(
        query_kernel, [(flat, BF16)], z, q, grad_num, grad_den, own, scratch=[held_both], flops=work, name="query"
    )
    (sent,) = call(
        carried_kernel, [space], y, sums, lanes, weights, query_grad, unread=1, scratch=[held_time, carry], name="carried"
    )
    z = exchange(sent, SPACE, OWNERS)
    key_grad, value_grad = call(
        key_kernel, [(flat, BF16), (flat, BF16)], k, v, z, scratch=[held_space], flops=2 * work, name="key"
    )
    return query_grad.reshape(shape), key_grad.reshape(shape), value_grad.reshape(shape)


def solution(mesh):
    tokens = P("tm", "row", "col", None)
    return jax.shard_map(
        per_device,
        mesh=mesh,
        in_specs=(tokens, tokens, tokens, tokens, P("tm", None), P()),
        out_specs=(tokens, tokens, tokens),
        check_vma=False,
    )
```

```python
import jax
import jax.numpy as jnp
from jax import lax
from jax.experimental import pallas as pl
from jax.experimental.pallas import tpu as pltpu
from jax.sharding import PartitionSpec as P

HEADS = 36
DIM = 32
LANES = 128
GROUPS = HEADS * DIM // LANES
PER_GROUP = LANES // DIM
FRAMES = 2
ROWS = 8
COLS = 16
TOKENS = ROWS * COLS
CH = HEADS * DIM
OWNERS = 16
HALF = DIM // 2
STATES = 2 * GROUPS
EXTRA = STATES + GROUPS
SLOTS = EXTRA + 1
OWNED = FRAMES * SLOTS
BOTH = 2 * FRAMES * STATES
PIECE = 64
PIECES = FRAMES * TOKENS // PIECE
SPACE = ("row", "col")
VMEM_BYTES = 16 * 1024 * 1024
WIDE_BYTES = 60 * 1024 * 1024
F32 = jnp.float32
BF16 = jnp.bfloat16


def call(body, outs, *args, far=0, unread=0, far_outs=0, scratch=(), flops=1_000_000, vmem=VMEM_BYTES, name=None):
    out_shape = tuple(jax.ShapeDtypeStruct(shape, dtype) for shape, dtype in outs)
    moved = sum(a.size * a.dtype.itemsize for a in args) + sum(o.size * o.dtype.itemsize for o in out_shape)
    near, away = pl.BlockSpec(memory_space=pltpu.VMEM), pl.BlockSpec(memory_space=pltpu.HBM)
    return pl.pallas_call(
        body,
        out_shape=out_shape,
        in_specs=[near] * (len(args) - far - unread) + [away] * far + [pl.BlockSpec(memory_space=pl.ANY)] * unread,
        out_specs=tuple([near] * (len(outs) - far_outs) + [away] * far_outs),
        scratch_shapes=list(scratch),
        compiler_params=pltpu.CompilerParams(vmem_limit_bytes=vmem),
        cost_estimate=pl.CostEstimate(flops=flops, bytes_accessed=moved, transcendentals=0),
        name=name,
    )(*args)


def dot(a, b, contract=((1,), (0,)), precision=None):
    return lax.dot_general(a, b, (contract, ((), ())), preferred_element_type=F32, precision=precision)


def iota(shape, dim):
    return lax.broadcasted_iota(jnp.int32, shape, dim)


def lane_head(shape):
    return iota(shape, 1) // DIM


def compact(square):
    head = lane_head((DIM, LANES))
    out = square[(PER_GROUP - 1) * DIM :]
    for i in reversed(range(PER_GROUP - 1)):
        out = jnp.where(head == i, square[i * DIM : (i + 1) * DIM], out)
    return out


def spread(rows):
    head = lane_head((DIM, LANES))
    return jnp.concatenate([jnp.where(head == i, rows, 0.0) for i in range(PER_GROUP)], axis=0).astype(BF16)


def head_ones():
    return (iota((LANES, LANES), 0) // DIM == lane_head((LANES, LANES))).astype(BF16)


def put_rows(held, size, start, rows):
    for half in range(2):
        held[pl.ds(start + half * GROUPS, OWNERS, stride=size), :] = rows[half * HALF : (half + 1) * HALF]


def take_rows(held, size, start):
    return jnp.concatenate([held[pl.ds(start + half * GROUPS, OWNERS, stride=size), :] for half in range(2)], axis=0)


def part(ref, f, g):
    return ref[f * TOKENS : (f + 1) * TOKENS, g * LANES : (g + 1) * LANES]


def decay_kernel(decay_ref, lanes_ref, row_ref):
    decay = decay_ref[...]
    own = iota((SLOTS, HEADS), 1) // PER_GROUP == iota((SLOTS, HEADS), 0) % GROUPS
    onto = (iota((HEADS, LANES), 0) % PER_GROUP == lane_head((HEADS, LANES))).astype(F32)
    for f in range(FRAMES):
        picked = jnp.where(own, decay[f : f + 1], 0.0)
        lanes_ref[f * SLOTS : (f + 1) * SLOTS, :] = dot(picked, onto, precision=lax.Precision.HIGHEST)
    rest = jnp.broadcast_to(decay[0:1] * decay[1:2], (8, HEADS))
    row = jnp.zeros((8, LANES), F32)
    for third in range(3):
        piece = rest.astype(BF16)
        rest = rest - piece.astype(F32)
        row = row + dot(piece, (iota((HEADS, LANES), 1) == iota((HEADS, LANES), 0) + third * HEADS).astype(BF16))
    row_ref[...] = row


def update_kernel(k_ref, v_ref, out_ref, held, keys, values, sems):
    pieces = [
        [
            pltpu.make_async_copy(source.at[piece], target.at[piece], sems.at[i, j])
            for i, (source, target) in enumerate(((k_ref, keys), (v_ref, values)))
        ]
        for j, piece in enumerate(pl.ds(j * PIECE, PIECE) for j in range(PIECES))
    ]
    for piece in pieces:
        for move in piece:
            move.start()
    for f in range(FRAMES):
        held[pl.ds(f * SLOTS + EXTRA, OWNERS, stride=OWNED), :] = jnp.zeros((OWNERS, LANES), F32)
    for f in range(FRAMES):
        for piece in pieces[f * PIECES // FRAMES : (f + 1) * PIECES // FRAMES]:
            for move in piece:
                move.wait()
        for g in range(GROUPS):
            pos_k = jnp.maximum(part(keys, f, g), 0)
            put_rows(held, OWNED, f * SLOTS + g, compact(dot(pos_k, part(values, f, g), ((0,), (0,)))))
            normal = jnp.sum(pos_k.astype(F32), axis=0, keepdims=True)
            held[pl.ds(f * SLOTS + STATES + g, OWNERS, stride=OWNED), :] = jnp.broadcast_to(normal, (OWNERS, LANES))
    out_ref[...] = held[...].astype(BF16)


def frame_sums(x_ref):
    return jnp.sum(x_ref[...].astype(F32).reshape(OWNERS, OWNED, LANES), axis=0)


def copies(block, out_ref):
    count = out_ref.shape[0] // block.shape[0]
    out_ref[...] = jnp.broadcast_to(block[None], (count,) + block.shape).reshape(out_ref.shape).astype(BF16)


def block_forward_kernel(x_ref, lanes_ref, row_ref, sums_ref, out_ref):
    sums = frame_sums(x_ref)
    sums_ref[...] = sums
    total = lanes_ref[SLOTS:, :] * sums[:SLOTS] + sums[SLOTS:]
    total = jnp.where(iota((SLOTS, LANES), 0) == EXTRA, row_ref[0:1, :], total)
    copies(jnp.concatenate([total, total], axis=0), out_ref)


def shifted(x, by, count):
    row = iota(x.shape, 0)
    if by > 0:
        return jnp.where(row < by, 1.0, pltpu.roll(x, by, 0))
    return jnp.where(row >= count + by, 1.0, pltpu.roll(x, count + by, 0))


def block_weights(held, index, count, backward):
    mine = lax.axis_index("tm")
    decays = held[pl.ds(EXTRA, count, stride=SLOTS), :].astype(BF16)
    source = iota((LANES, LANES), 0)
    onto = (source < 3 * HEADS) & (source % HEADS == index * PER_GROUP + lane_head((LANES, LANES)))
    block = dot(decays, onto.astype(BF16))
    at = iota((count, LANES), 0)
    between = at > mine if backward else at < mine
    product = shifted(jnp.where(between, block, 1.0), 1 if backward else -1, count)
    step = 1
    while step < count:
        product = product * shifted(product, step if backward else -step, count)
        step *= 2
    return jnp.where(between, product, 0.0)


def entering(held, carry, weights, count):
    carry[EXTRA:SLOTS, :] = jnp.zeros((1, LANES), F32)
    for slot in range(EXTRA):
        rows = held[pl.ds(slot, count, stride=SLOTS), :]
        carry[slot : slot + 1, :] = jnp.sum(weights[slot % GROUPS] * rows, axis=0, keepdims=True)
    return carry[:SLOTS, :]


def around(x, before, after):
    at = iota(x.shape, 0)
    from_left = jnp.where(at == 0, before, pltpu.roll(x, 1, 0))
    from_right = jnp.where(at == COLS - 1, after, pltpu.roll(x, COLS - 1, 0))
    return from_right, x, from_left


def weighted(taps, row_off, cells):
    tap = (row_off + 1) * 3
    return taps[tap] * cells[0] + taps[tap + 1] * cells[1] + taps[tap + 2] * cells[2]


def from_row(ref, taps, row_off, f, lanes):
    corners = ref[FRAMES * COLS :, lanes].astype(F32)
    x = ref[f * COLS : (f + 1) * COLS, lanes].astype(F32)
    return weighted(taps, row_off, around(x, corners[2 * f : 2 * f + 1], corners[2 * f + 1 : 2 * f + 2]))


def states_kernel(
    y_ref,
    sums_ref,
    lanes_ref,
    q_ref,
    ga_ref,
    above_ref,
    below_ref,
    weight_ref,
    own_ref,
    inverse_ref,
    num_ref,
    out_ref,
    after_ref,
    held,
    carry,
    sent,
):
    count = y_ref.shape[0] // SLOTS
    held[...] = y_ref[...].astype(F32)
    weights = [block_weights(held, g, count, False) for g in range(GROUPS)]
    before = entering(held, carry, weights, count)
    for g in range(GROUPS):
        after_ref[g] = block_weights(held, g, count, True)
    first = lanes_ref[:SLOTS, :] * before + sums_ref[:SLOTS, :]
    second = lanes_ref[SLOTS:, :] * first + sums_ref[SLOTS:, :]
    own_ref[:SLOTS, :] = first
    own_ref[SLOTS:, :] = second
    for owner in range(OWNERS):
        sent[owner * BOTH : owner * BOTH + STATES, :] = first[:STATES]
        sent[owner * BOTH + STATES : owner * BOTH + 2 * STATES, :] = second[:STATES]
    ones = head_ones()
    for f in range(FRAMES):
        for g in range(GROUPS):
            normal = (first, second)[f][STATES + g : STATES + g + 1]
            pos_q = jnp.maximum(part(q_ref, f, g), 0)
            inverse = 1.0 / (dot((pos_q.astype(F32) * normal).astype(BF16), ones) + 1.0)
            lanes = slice(g * LANES, (g + 1) * LANES)
            taps = [weight_ref[t : t + 1, lanes] for t in range(9)]
            inner = part(ga_ref, f, g)
            top = inner[:COLS] + from_row(above_ref, taps, 1, f, lanes)
            bottom = inner[-COLS:] + from_row(below_ref, taps, -1, f, lanes)
            grad_attn = jnp.concatenate([top, inner[COLS:-COLS], bottom], axis=0)
            grad_num = (grad_attn * inverse).astype(BF16)
            here = (slice(f * TOKENS, (f + 1) * TOKENS), slice(g * LANES, (g + 1) * LANES))
            inverse_ref[here] = inverse
            num_ref[here] = grad_num
            put_rows(sent, BOTH, (FRAMES + f) * STATES + g, compact(dot(pos_q, grad_num, ((0,), (0,)))))
    out_ref[...] = sent[...].astype(BF16)


def locals_kernel(z_ref, q_ref, num_ref, inverse_ref, lanes_ref, sums_ref, den_ref, out_ref, held):
    held[...] = z_ref[...].astype(F32)
    sums = jnp.sum(z_ref[...].astype(F32).reshape(OWNERS, BOTH, LANES), axis=0)
    ones = head_ones()
    lane = iota((TOKENS, LANES), 1) % DIM
    for f in range(FRAMES):
        sums_ref[f * SLOTS : f * SLOTS + STATES, :] = sums[(FRAMES + f) * STATES : (FRAMES + f + 1) * STATES]
        sums_ref[f * SLOTS + EXTRA : (f + 1) * SLOTS, :] = jnp.zeros((1, LANES), F32)
        packed = jnp.zeros((TOKENS, LANES), F32)
        for g in range(GROUPS):
            state = spread(take_rows(held, BOTH, f * STATES + g))
            pos_q = jnp.maximum(part(q_ref, f, g), 0)
            product = part(num_ref, f, g).astype(F32) * dot(pos_q, state)
            grad_den = -dot(product.astype(BF16), ones) * part(inverse_ref, f, g)
            packed = packed + jnp.where(lane == g, grad_den, 0.0)
            at = f * SLOTS + STATES + g
            sums_ref[at : at + 1, :] = jnp.sum(grad_den * pos_q.astype(F32), axis=0, keepdims=True)
        den_ref[f * TOKENS : (f + 1) * TOKENS, :] = packed.astype(BF16)
    total = lanes_ref[:SLOTS, :] * (sums_ref[:SLOTS, :] + lanes_ref[SLOTS:, :] * sums_ref[SLOTS:, :])
    copies(jnp.concatenate([total, total], axis=0), out_ref)


def query_kernel(z_ref, q_ref, num_ref, den_ref, own_ref, grad_ref, held):
    held[...] = z_ref[...].astype(F32)
    source = iota((LANES, LANES), 0)
    same = source // DIM == lane_head((LANES, LANES))
    for f in range(FRAMES):
        den = den_ref[f * TOKENS : (f + 1) * TOKENS, :]
        for g in range(GROUPS):
            state = spread(take_rows(held, BOTH, f * STATES + g))
            at = f * SLOTS + STATES + g
            here = (slice(f * TOKENS, (f + 1) * TOKENS), slice(g * LANES, (g + 1) * LANES))
            grad_den = dot(den, (same & (source % DIM == g)).astype(BF16))
            grad = dot(num_ref[here], state, ((1,), (1,))) + grad_den * own_ref[at : at + 1, :]
            grad_ref[here] = jnp.where(q_ref[here].astype(F32) > 0, grad, 0.0).astype(BF16)


def carried_kernel(y_ref, sums_ref, lanes_ref, weights_ref, out_ref, held, carry):
    count = y_ref.shape[0] // SLOTS
    held[...] = y_ref[...].astype(F32)
    after = entering(held, carry, [weights_ref[g] for g in range(GROUPS)], count)
    second = sums_ref[SLOTS:, :] + after
    first = sums_ref[:SLOTS, :] + lanes_ref[SLOTS:, :] * second
    copies(jnp.concatenate([first, second], axis=0), out_ref)


def edge_cols_kernel(g_ref, first_ref, last_ref, first, last):
    for at in range(FRAMES * ROWS):
        x = g_ref[at * COLS : (at + 1) * COLS, :].astype(F32)
        first[at : at + 1, :] = x[:1]
        last[at : at + 1, :] = x[COLS - 1 :]
    first_ref[...] = first[...].astype(BF16)
    last_ref[...] = last[...].astype(BF16)


def edge_rows_kernel(g_ref, left_ref, right_ref, first_ref, last_ref, corners):
    left = left_ref[...].astype(F32)
    right = right_ref[...].astype(F32)
    for out_ref, row in ((first_ref, 0), (last_ref, ROWS - 1)):
        corners[...] = jnp.zeros(corners.shape, F32)
        for f in range(FRAMES):
            at = f * ROWS + row
            out_ref[f * COLS : (f + 1) * COLS, :] = g_ref[at * COLS : (at + 1) * COLS, :]
            corners[2 * f : 2 * f + 1, :] = left[at : at + 1]
            corners[2 * f + 1 : 2 * f + 2, :] = right[at : at + 1]
        out_ref[FRAMES * COLS :, :] = corners[...].astype(BF16)


def conv_kernel(g_ref, left_ref, right_ref, weight_ref, out_ref):
    left = left_ref[...].astype(F32)
    right = right_ref[...].astype(F32)
    for f in range(FRAMES):
        for g in range(GROUPS):
            lanes = slice(g * LANES, (g + 1) * LANES)
            taps = [weight_ref[t : t + 1, lanes] for t in range(9)]
            total = [None] * ROWS
            for source in range(ROWS):
                first = f * ROWS + source
                x = g_ref[first * COLS : (first + 1) * COLS, lanes].astype(F32)
                cells = around(x, left[first : first + 1, lanes], right[first : first + 1, lanes])
                for row_off in (-1, 0, 1):
                    row = source + row_off
                    if 0 <= row < ROWS:
                        add = weighted(taps, row_off, cells)
                        if row_off == 0:
                            add = add + x
                        total[row] = add if total[row] is None else total[row] + add
            for row in range(ROWS):
                first = (f * ROWS + row) * COLS
                out_ref[first : first + COLS, lanes] = total[row]


def key_kernel(k_ref, v_ref, z_ref, key_grad_ref, value_grad_ref, held, key_grad, value_grad, sems):
    held[...] = z_ref[...].astype(F32)
    sums = frame_sums(z_ref)
    moves = []
    for f in range(FRAMES):
        for g in range(GROUPS):
            carried = spread(take_rows(held, OWNED, f * SLOTS + g))
            at = f * SLOTS + STATES + g
            keys = part(k_ref, f, g)
            here = (slice(f * TOKENS, (f + 1) * TOKENS), slice(g * LANES, (g + 1) * LANES))
            grad = dot(part(v_ref, f, g), carried, ((1,), (1,))) + sums[at : at + 1]
            key_grad[here] = jnp.where(keys.astype(F32) > 0, grad, 0.0).astype(BF16)
            value_grad[here] = dot(jnp.maximum(keys, 0), carried).astype(BF16)
        for j in range(f * PIECES // FRAMES, (f + 1) * PIECES // FRAMES):
            piece = pl.ds(j * PIECE, PIECE)
            for i, (source, target) in enumerate(((key_grad, key_grad_ref), (value_grad, value_grad_ref))):
                move = pltpu.make_async_copy(source.at[piece], target.at[piece], sems.at[i, j])
                move.start()
                moves.append(move)
    for move in moves:
        move.wait()


def exchange(block, axes, count):
    rows = block.shape[0] // count
    block = block.reshape(count, rows // 2, 2, LANES)
    return lax.all_to_all(block, axes, 0, 0, tiled=True).reshape(count * rows, LANES)


def neighbours(first, last, axis):
    count = lax.axis_size(axis)
    before = lax.ppermute(last, axis, [(i, i + 1) for i in range(count - 1)])
    after = lax.ppermute(first, axis, [(i + 1, i) for i in range(count - 1)])
    return before, after


def per_device(query_tokens, key_tokens, value_tokens, grad_output, frame_decay, conv_weight):
    shape = query_tokens.shape
    flat = (FRAMES * TOKENS, CH)
    blocks = lax.axis_size("tm")
    q, k, v, g = (x.reshape(flat) for x in (query_tokens, key_tokens, value_tokens, grad_output))
    space = ((OWNERS * OWNED, LANES), BF16)
    both = ((OWNERS * BOTH, LANES), BF16)
    time = ((blocks * SLOTS, LANES), BF16)
    owned = ((OWNED, LANES), F32)
    held_space, held_both, held_time = (pltpu.VMEM(kind[0], F32) for kind in (space, both, time))
    carry = pltpu.VMEM((32, LANES), F32)
    work = 2 * FRAMES * GROUPS * TOKENS * LANES * LANES

    buffer = pltpu.VMEM(flat, BF16)
    copies_done = pltpu.SemaphoreType.DMA((2, PIECES))
    (sent,) = call(
        update_kernel,
        [space],
        k,
        v,
        far=2,
        scratch=[held_space, buffer, buffer, copies_done],
        flops=work,
        vmem=WIDE_BYTES,
        name="update",
    )
    lanes, decay_row = call(decay_kernel, [owned, ((8, LANES), F32)], frame_decay, name="decay")
    x = exchange(sent, SPACE, OWNERS)
    side = ((FRAMES * ROWS, CH), BF16)
    edge = ((FRAMES * COLS + 16, CH), BF16)
    held_side = pltpu.VMEM(side[0], F32)
    first, last = call(edge_cols_kernel, [side, side], g, scratch=[held_side, held_side], name="edge_cols")
    left, right = neighbours(first, last, "col")
    first, last = call(edge_rows_kernel, [edge, edge], g, left, right, scratch=[held_side], flops=20_000_000_000, name="edge_rows")
    above, below = neighbours(first, last, "row")
    sums, sent = call(block_forward_kernel, [owned, time], x, lanes, decay_row, name="block_forward")
    y = exchange(sent, "tm", blocks)
    (grad_attn,) = call(
        conv_kernel, [(flat, F32)], g, left, right, conv_weight, flops=20 * flat[0] * flat[1], name="conv"
    )
    own, inverse, grad_num, sent, weights = call(
        states_kernel,
        [owned, (flat, F32), (flat, BF16), both, ((GROUPS, blocks, LANES), F32)],
        y,
        sums,
        lanes,
        q,
        grad_attn,
        above,
        below,
        conv_weight,
        scratch=[held_time, carry, held_both],
        flops=2 * work,
        name="states",
    )
    z = exchange(sent, SPACE, OWNERS)
    sums, grad_den, sent = call(
        locals_kernel,
        [owned, ((FRAMES * TOKENS, LANES), BF16), time],
        z,
        q,
        grad_num,
        inverse,
        lanes,
        scratch=[held_both],
        flops=2 * work,
        name="locals",
    )
    y = exchange(sent, "tm", blocks)
    (query_grad,) = call(
        query_kernel, [(flat, BF16)], z, q, grad_num, grad_den, own, scratch=[held_both], flops=work, name="query"
    )
    (sent,) = call(carried_kernel, [space], y, sums, lanes, weights, scratch=[held_time, carry], name="carried")
    z = exchange(sent, SPACE, OWNERS)
    key_grad, value_grad = call(
        key_kernel,
        [(flat, BF16), (flat, BF16)],
        k,
        v,
        z,
        far_outs=2,
        scratch=[held_space, buffer, buffer, copies_done],
        flops=2 * work,
        name="key",
    )
    return query_grad.reshape(shape), key_grad.reshape(shape), value_grad.reshape(shape)


def solution(mesh):
    tokens = P("tm", "row", "col", None)
    return jax.shard_map(
        per_device,
        mesh=mesh,
        in_specs=(tokens, tokens, tokens, tokens, P("tm", None), P()),
        out_specs=(tokens, tokens, tokens),
        check_vma=False,
    )
```

```python
import jax
import jax.numpy as jnp
from jax import lax
from jax.experimental import pallas as pl
from jax.experimental.pallas import tpu as pltpu
from jax.sharding import PartitionSpec as P

HEADS = 36
DIM = 32
LANES = 128
GROUPS = HEADS * DIM // LANES
PER_GROUP = LANES // DIM
FRAMES = 2
ROWS = 8
COLS = 16
TOKENS = ROWS * COLS
CH = HEADS * DIM
OWNERS = 16
HALF = DIM // 2
STATES = 2 * GROUPS
EXTRA = STATES + GROUPS
SLOTS = EXTRA + 1
OWNED = FRAMES * SLOTS
BOTH = 2 * FRAMES * STATES
PIECE = 128
PIECES = FRAMES * TOKENS // PIECE
SPACE = ("row", "col")
VMEM_BYTES = 16 * 1024 * 1024
WIDE_BYTES = 60 * 1024 * 1024
F32 = jnp.float32
BF16 = jnp.bfloat16


def call(body, outs, *args, far=0, unread=0, far_outs=0, scratch=(), flops=1_000_000, vmem=VMEM_BYTES, name=None):
    out_shape = tuple(jax.ShapeDtypeStruct(shape, dtype) for shape, dtype in outs)
    moved = sum(a.size * a.dtype.itemsize for a in args) + sum(o.size * o.dtype.itemsize for o in out_shape)
    near, away = pl.BlockSpec(memory_space=pltpu.VMEM), pl.BlockSpec(memory_space=pltpu.HBM)
    return pl.pallas_call(
        body,
        out_shape=out_shape,
        in_specs=[near] * (len(args) - far - unread) + [away] * far + [pl.BlockSpec(memory_space=pl.ANY)] * unread,
        out_specs=tuple([near] * (len(outs) - far_outs) + [away] * far_outs),
        scratch_shapes=list(scratch),
        compiler_params=pltpu.CompilerParams(vmem_limit_bytes=vmem),
        cost_estimate=pl.CostEstimate(flops=flops, bytes_accessed=moved, transcendentals=0),
        name=name,
    )(*args)


def dot(a, b, contract=((1,), (0,)), precision=None):
    return lax.dot_general(a, b, (contract, ((), ())), preferred_element_type=F32, precision=precision)


def iota(shape, dim):
    return lax.broadcasted_iota(jnp.int32, shape, dim)


def lane_head(shape):
    return iota(shape, 1) // DIM


def compact(square):
    head = lane_head((DIM, LANES))
    out = square[(PER_GROUP - 1) * DIM :]
    for i in reversed(range(PER_GROUP - 1)):
        out = jnp.where(head == i, square[i * DIM : (i + 1) * DIM], out)
    return out


def spread(rows):
    head = lane_head((DIM, LANES))
    return jnp.concatenate([jnp.where(head == i, rows, 0.0) for i in range(PER_GROUP)], axis=0).astype(BF16)


def head_ones():
    return (iota((LANES, LANES), 0) // DIM == lane_head((LANES, LANES))).astype(BF16)


def put_rows(held, size, start, rows):
    for half in range(2):
        held[pl.ds(start + half * GROUPS, OWNERS, stride=size), :] = rows[half * HALF : (half + 1) * HALF]


def take_rows(held, size, start):
    return jnp.concatenate([held[pl.ds(start + half * GROUPS, OWNERS, stride=size), :] for half in range(2)], axis=0)


def part(ref, f, g):
    return ref[f * TOKENS : (f + 1) * TOKENS, g * LANES : (g + 1) * LANES]


def decay_kernel(decay_ref, lanes_ref, row_ref):
    decay = decay_ref[...]
    own = iota((SLOTS, HEADS), 1) // PER_GROUP == iota((SLOTS, HEADS), 0) % GROUPS
    onto = (iota((HEADS, LANES), 0) % PER_GROUP == lane_head((HEADS, LANES))).astype(F32)
    for f in range(FRAMES):
        picked = jnp.where(own, decay[f : f + 1], 0.0)
        lanes_ref[f * SLOTS : (f + 1) * SLOTS, :] = dot(picked, onto, precision=lax.Precision.HIGHEST)
    rest = jnp.broadcast_to(decay[0:1] * decay[1:2], (8, HEADS))
    row = jnp.zeros((8, LANES), F32)
    for third in range(3):
        piece = rest.astype(BF16)
        rest = rest - piece.astype(F32)
        row = row + dot(piece, (iota((HEADS, LANES), 1) == iota((HEADS, LANES), 0) + third * HEADS).astype(BF16))
    row_ref[...] = row


def update_kernel(k_ref, v_ref, out_ref, held, keys, values, sems):
    pieces = [
        [
            pltpu.make_async_copy(source.at[piece], target.at[piece], sems.at[i, j])
            for i, (source, target) in enumerate(((k_ref, keys), (v_ref, values)))
        ]
        for j, piece in enumerate(pl.ds(j * PIECE, PIECE) for j in range(PIECES))
    ]
    for piece in pieces:
        for move in piece:
            move.start()
    for f in range(FRAMES):
        held[pl.ds(f * SLOTS + EXTRA, OWNERS, stride=OWNED), :] = jnp.zeros((OWNERS, LANES), F32)
    for f in range(FRAMES):
        for piece in pieces[f * PIECES // FRAMES : (f + 1) * PIECES // FRAMES]:
            for move in piece:
                move.wait()
        for g in range(GROUPS):
            pos_k = jnp.maximum(part(keys, f, g), 0)
            put_rows(held, OWNED, f * SLOTS + g, compact(dot(pos_k, part(values, f, g), ((0,), (0,)))))
            normal = jnp.sum(pos_k.astype(F32), axis=0, keepdims=True)
            held[pl.ds(f * SLOTS + STATES + g, OWNERS, stride=OWNED), :] = jnp.broadcast_to(normal, (OWNERS, LANES))
    out_ref[...] = held[...].astype(BF16)


def frame_sums(x_ref):
    return jnp.sum(x_ref[...].astype(F32).reshape(OWNERS, OWNED, LANES), axis=0)


def copies(block, out_ref):
    count = out_ref.shape[0] // block.shape[0]
    out_ref[...] = jnp.broadcast_to(block[None], (count,) + block.shape).reshape(out_ref.shape).astype(BF16)


def block_forward_kernel(x_ref, lanes_ref, row_ref, sums_ref, out_ref):
    sums = frame_sums(x_ref)
    sums_ref[...] = sums
    total = lanes_ref[SLOTS:, :] * sums[:SLOTS] + sums[SLOTS:]
    total = jnp.where(iota((SLOTS, LANES), 0) == EXTRA, row_ref[0:1, :], total)
    copies(jnp.concatenate([total, total], axis=0), out_ref)


def shifted(x, by, count):
    row = iota(x.shape, 0)
    if by > 0:
        return jnp.where(row < by, 1.0, pltpu.roll(x, by, 0))
    return jnp.where(row >= count + by, 1.0, pltpu.roll(x, count + by, 0))


def block_weights(held, index, count, backward):
    mine = lax.axis_index("tm")
    decays = held[pl.ds(EXTRA, count, stride=SLOTS), :].astype(BF16)
    source = iota((LANES, LANES), 0)
    onto = (source < 3 * HEADS) & (source % HEADS == index * PER_GROUP + lane_head((LANES, LANES)))
    block = dot(decays, onto.astype(BF16))
    at = iota((count, LANES), 0)
    between = at > mine if backward else at < mine
    product = shifted(jnp.where(between, block, 1.0), 1 if backward else -1, count)
    step = 1
    while step < count:
        product = product * shifted(product, step if backward else -step, count)
        step *= 2
    return jnp.where(between, product, 0.0)


def entering(held, carry, weights, count):
    carry[EXTRA:SLOTS, :] = jnp.zeros((1, LANES), F32)
    for slot in range(EXTRA):
        rows = held[pl.ds(slot, count, stride=SLOTS), :]
        carry[slot : slot + 1, :] = jnp.sum(weights[slot % GROUPS] * rows, axis=0, keepdims=True)
    return carry[:SLOTS, :]


def around(x, before, after):
    at = iota(x.shape, 0)
    from_left = jnp.where(at == 0, before, pltpu.roll(x, 1, 0))
    from_right = jnp.where(at == COLS - 1, after, pltpu.roll(x, COLS - 1, 0))
    return from_right, x, from_left


def weighted(taps, row_off, cells):
    tap = (row_off + 1) * 3
    return taps[tap] * cells[0] + taps[tap + 1] * cells[1] + taps[tap + 2] * cells[2]


def from_row(edge, taps, row_off, f):
    corners = edge[FRAMES * COLS :]
    x = edge[f * COLS : (f + 1) * COLS]
    return weighted(taps, row_off, around(x, corners[2 * f : 2 * f + 1], corners[2 * f + 1 : 2 * f + 2]))


def states_kernel(
    y_ref,
    sums_ref,
    lanes_ref,
    q_ref,
    ga_ref,
    pair_ref,
    next_ref,
    weight_ref,
    own_ref,
    inverse_ref,
    num_ref,
    out_ref,
    after_ref,
    held,
    carry,
    sent,
):
    count = y_ref.shape[0] // SLOTS
    held[...] = y_ref[...].astype(F32)
    weights = [block_weights(held, g, count, False) for g in range(GROUPS)]
    before = entering(held, carry, weights, count)
    for g in range(GROUPS):
        after_ref[g] = block_weights(held, g, count, True)
    first = lanes_ref[:SLOTS, :] * before + sums_ref[:SLOTS, :]
    second = lanes_ref[SLOTS:, :] * first + sums_ref[SLOTS:, :]
    own_ref[:SLOTS, :] = first
    own_ref[SLOTS:, :] = second
    for owner in range(OWNERS):
        sent[owner * BOTH : owner * BOTH + STATES, :] = first[:STATES]
        sent[owner * BOTH + STATES : owner * BOTH + 2 * STATES, :] = second[:STATES]
    ones = head_ones()
    for f in range(FRAMES):
        for g in range(GROUPS):
            normal = (first, second)[f][STATES + g : STATES + g + 1]
            pos_q = jnp.maximum(part(q_ref, f, g), 0)
            inverse = 1.0 / (dot((pos_q.astype(F32) * normal).astype(BF16), ones) + 1.0)
            lanes = slice(g * LANES, (g + 1) * LANES)
            taps = [weight_ref[t : t + 1, lanes] for t in range(9)]
            inner = part(ga_ref, f, g)
            above, below = swapped("row", pair_ref[:, lanes].astype(F32), next_ref[:, lanes].astype(F32))
            top = inner[:COLS] + from_row(above, taps, 1, f)
            bottom = inner[-COLS:] + from_row(below, taps, -1, f)
            grad_attn = jnp.concatenate([top, inner[COLS:-COLS], bottom], axis=0)
            grad_num = (grad_attn * inverse).astype(BF16)
            here = (slice(f * TOKENS, (f + 1) * TOKENS), slice(g * LANES, (g + 1) * LANES))
            inverse_ref[here] = inverse
            num_ref[here] = grad_num
            put_rows(sent, BOTH, (FRAMES + f) * STATES + g, compact(dot(pos_q, grad_num, ((0,), (0,)))))
    out_ref[...] = sent[...].astype(BF16)


def locals_kernel(z_ref, q_ref, num_ref, inverse_ref, lanes_ref, sums_ref, den_ref, out_ref, held):
    held[...] = z_ref[...].astype(F32)
    sums = jnp.sum(z_ref[...].astype(F32).reshape(OWNERS, BOTH, LANES), axis=0)
    ones = head_ones()
    lane = iota((TOKENS, LANES), 1) % DIM
    for f in range(FRAMES):
        sums_ref[f * SLOTS : f * SLOTS + STATES, :] = sums[(FRAMES + f) * STATES : (FRAMES + f + 1) * STATES]
        sums_ref[f * SLOTS + EXTRA : (f + 1) * SLOTS, :] = jnp.zeros((1, LANES), F32)
        packed = jnp.zeros((TOKENS, LANES), F32)
        for g in range(GROUPS):
            state = spread(take_rows(held, BOTH, f * STATES + g))
            pos_q = jnp.maximum(part(q_ref, f, g), 0)
            product = part(num_ref, f, g).astype(F32) * dot(pos_q, state)
            grad_den = -dot(product.astype(BF16), ones) * part(inverse_ref, f, g)
            packed = packed + jnp.where(lane == g, grad_den, 0.0)
            at = f * SLOTS + STATES + g
            sums_ref[at : at + 1, :] = jnp.sum(grad_den * pos_q.astype(F32), axis=0, keepdims=True)
        den_ref[f * TOKENS : (f + 1) * TOKENS, :] = packed.astype(BF16)
    total = lanes_ref[:SLOTS, :] * (sums_ref[:SLOTS, :] + lanes_ref[SLOTS:, :] * sums_ref[SLOTS:, :])
    copies(jnp.concatenate([total, total], axis=0), out_ref)


def query_kernel(z_ref, q_ref, num_ref, den_ref, own_ref, grad_ref, held):
    held[...] = z_ref[...].astype(F32)
    source = iota((LANES, LANES), 0)
    same = source // DIM == lane_head((LANES, LANES))
    for f in range(FRAMES):
        den = den_ref[f * TOKENS : (f + 1) * TOKENS, :]
        for g in range(GROUPS):
            state = spread(take_rows(held, BOTH, f * STATES + g))
            at = f * SLOTS + STATES + g
            here = (slice(f * TOKENS, (f + 1) * TOKENS), slice(g * LANES, (g + 1) * LANES))
            grad_den = dot(den, (same & (source % DIM == g)).astype(BF16))
            grad = dot(num_ref[here], state, ((1,), (1,))) + grad_den * own_ref[at : at + 1, :]
            grad_ref[here] = jnp.where(q_ref[here].astype(F32) > 0, grad, 0.0).astype(BF16)


def carried_kernel(y_ref, sums_ref, lanes_ref, weights_ref, out_ref, held, carry):
    count = y_ref.shape[0] // SLOTS
    held[...] = y_ref[...].astype(F32)
    after = entering(held, carry, [weights_ref[g] for g in range(GROUPS)], count)
    second = sums_ref[SLOTS:, :] + after
    first = sums_ref[:SLOTS, :] + lanes_ref[SLOTS:, :] * second
    copies(jnp.concatenate([first, second], axis=0), out_ref)


def swapped(axis, first, second):
    odd = lax.axis_index(axis) % 2 == 1
    return jnp.where(odd, first, second), jnp.where(odd, second, first)


def edge_cols_kernel(g_ref, inner_ref, outer_ref, first, last):
    for at in range(FRAMES * ROWS):
        x = g_ref[at * COLS : (at + 1) * COLS, :].astype(F32)
        first[at : at + 1, :] = x[:1]
        last[at : at + 1, :] = x[COLS - 1 :]
    inner, outer = swapped("col", first[...], last[...])
    inner_ref[...] = inner.astype(BF16)
    outer_ref[...] = outer.astype(BF16)


def edge_rows_kernel(g_ref, pair_ref, next_ref, inner_ref, outer_ref, corners):
    left, right = swapped("col", pair_ref[...].astype(F32), next_ref[...].astype(F32))
    edges = []
    for row in (0, ROWS - 1):
        corners[...] = jnp.zeros(corners.shape, F32)
        cells = []
        for f in range(FRAMES):
            at = f * ROWS + row
            cells.append(g_ref[at * COLS : (at + 1) * COLS, :].astype(F32))
            corners[2 * f : 2 * f + 1, :] = left[at : at + 1]
            corners[2 * f + 1 : 2 * f + 2, :] = right[at : at + 1]
        edges.append(jnp.concatenate(cells + [corners[...]], axis=0))
    inner, outer = swapped("row", *edges)
    inner_ref[...] = inner.astype(BF16)
    outer_ref[...] = outer.astype(BF16)


def conv_kernel(g_ref, pair_ref, next_ref, weight_ref, out_ref):
    left, right = swapped("col", pair_ref[...].astype(F32), next_ref[...].astype(F32))
    for f in range(FRAMES):
        for g in range(GROUPS):
            lanes = slice(g * LANES, (g + 1) * LANES)
            taps = [weight_ref[t : t + 1, lanes] for t in range(9)]
            total = [None] * ROWS
            for source in range(ROWS):
                first = f * ROWS + source
                x = g_ref[first * COLS : (first + 1) * COLS, lanes].astype(F32)
                cells = around(x, left[first : first + 1, lanes], right[first : first + 1, lanes])
                for row_off in (-1, 0, 1):
                    row = source + row_off
                    if 0 <= row < ROWS:
                        add = weighted(taps, row_off, cells)
                        if row_off == 0:
                            add = add + x
                        total[row] = add if total[row] is None else total[row] + add
            for row in range(ROWS):
                first = (f * ROWS + row) * COLS
                out_ref[first : first + COLS, lanes] = total[row]


def key_kernel(k_ref, v_ref, z_ref, key_grad_ref, value_grad_ref, held, key_grad, value_grad, sems):
    held[...] = z_ref[...].astype(F32)
    sums = frame_sums(z_ref)
    moves = []
    for f in range(FRAMES):
        for g in range(GROUPS):
            carried = spread(take_rows(held, OWNED, f * SLOTS + g))
            at = f * SLOTS + STATES + g
            keys = part(k_ref, f, g)
            here = (slice(f * TOKENS, (f + 1) * TOKENS), slice(g * LANES, (g + 1) * LANES))
            grad = dot(part(v_ref, f, g), carried, ((1,), (1,))) + sums[at : at + 1]
            key_grad[here] = jnp.where(keys.astype(F32) > 0, grad, 0.0).astype(BF16)
            value_grad[here] = dot(jnp.maximum(keys, 0), carried).astype(BF16)
        for j in range(f * PIECES // FRAMES, (f + 1) * PIECES // FRAMES):
            piece = pl.ds(j * PIECE, PIECE)
            for i, (source, target) in enumerate(((key_grad, key_grad_ref), (value_grad, value_grad_ref))):
                move = pltpu.make_async_copy(source.at[piece], target.at[piece], sems.at[i, j])
                move.start()
                moves.append(move)
    for move in moves:
        move.wait()


def exchange(block, axes, count):
    rows = block.shape[0] // count
    block = block.reshape(count, rows // 2, 2, LANES)
    return lax.all_to_all(block, axes, 0, 0, tiled=True).reshape(count * rows, LANES)


def neighbours(inner, outer, axis):
    count = lax.axis_size(axis)
    pairs = [[(i, i + 1) for i in range(start, count - 1, 2)] for start in range(2)]
    return tuple(
        lax.ppermute(edge, axis, [way for a, b in pair for way in ((a, b), (b, a))])
        for edge, pair in zip((inner, outer), pairs)
    )


def per_device(query_tokens, key_tokens, value_tokens, grad_output, frame_decay, conv_weight):
    shape = query_tokens.shape
    flat = (FRAMES * TOKENS, CH)
    blocks = lax.axis_size("tm")
    q, k, v, g = (x.reshape(flat) for x in (query_tokens, key_tokens, value_tokens, grad_output))
    space = ((OWNERS * OWNED, LANES), BF16)
    both = ((OWNERS * BOTH, LANES), BF16)
    time = ((blocks * SLOTS, LANES), BF16)
    owned = ((OWNED, LANES), F32)
    held_space, held_both, held_time = (pltpu.VMEM(kind[0], F32) for kind in (space, both, time))
    carry = pltpu.VMEM((32, LANES), F32)
    work = 2 * FRAMES * GROUPS * TOKENS * LANES * LANES

    buffer = pltpu.VMEM(flat, BF16)
    copies_done = pltpu.SemaphoreType.DMA((2, PIECES))
    (sent,) = call(
        update_kernel,
        [space],
        k,
        v,
        far=2,
        scratch=[held_space, buffer, buffer, copies_done],
        flops=work,
        vmem=WIDE_BYTES,
        name="update",
    )
    lanes, decay_row = call(decay_kernel, [owned, ((8, LANES), F32)], frame_decay, name="decay")
    x = exchange(sent, SPACE, OWNERS)
    side = ((FRAMES * ROWS, CH), BF16)
    edge = ((FRAMES * COLS + 16, CH), BF16)
    held_side = pltpu.VMEM(side[0], F32)
    inner, outer = call(edge_cols_kernel, [side, side], g, scratch=[held_side, held_side], name="edge_cols")
    beside = neighbours(inner, outer, "col")
    inner, outer = call(
        edge_rows_kernel, [edge, edge], g, *beside, scratch=[held_side], flops=20_000_000_000, name="edge_rows"
    )
    across = neighbours(inner, outer, "row")
    sums, sent = call(block_forward_kernel, [owned, time], x, lanes, decay_row, name="block_forward")
    y = exchange(sent, "tm", blocks)
    (grad_attn,) = call(
        conv_kernel, [(flat, F32)], g, *beside, conv_weight, flops=20 * flat[0] * flat[1], name="conv"
    )
    own, inverse, grad_num, sent, weights = call(
        states_kernel,
        [owned, (flat, F32), (flat, BF16), both, ((GROUPS, blocks, LANES), F32)],
        y,
        sums,
        lanes,
        q,
        grad_attn,
        *across,
        conv_weight,
        scratch=[held_time, carry, held_both],
        flops=2 * work,
        name="states",
    )
    z = exchange(sent, SPACE, OWNERS)
    sums, grad_den, sent = call(
        locals_kernel,
        [owned, ((FRAMES * TOKENS, LANES), BF16), time],
        z,
        q,
        grad_num,
        inverse,
        lanes,
        scratch=[held_both],
        flops=2 * work,
        name="locals",
    )
    y = exchange(sent, "tm", blocks)
    (query_grad,) = call(
        query_kernel, [(flat, BF16)], z, q, grad_num, grad_den, own, scratch=[held_both], flops=work, name="query"
    )
    (sent,) = call(carried_kernel, [space], y, sums, lanes, weights, scratch=[held_time, carry], name="carried")
    z = exchange(sent, SPACE, OWNERS)
    key_grad, value_grad = call(
        key_kernel,
        [(flat, BF16), (flat, BF16)],
        k,
        v,
        z,
        far_outs=2,
        scratch=[held_space, buffer, buffer, copies_done],
        flops=2 * work,
        name="key",
    )
    return query_grad.reshape(shape), key_grad.reshape(shape), value_grad.reshape(shape)


def solution(mesh):
    tokens = P("tm", "row", "col", None)
    return jax.shard_map(
        per_device,
        mesh=mesh,
        in_specs=(tokens, tokens, tokens, tokens, P("tm", None), P()),
        out_specs=(tokens, tokens, tokens),
        check_vma=False,
    )
```

```python
import jax
import jax.numpy as jnp
from jax import lax
from jax.experimental import pallas as pl
from jax.experimental.pallas import tpu as pltpu
from jax.sharding import PartitionSpec as P

HEADS = 36
DIM = 32
LANES = 128
GROUPS = HEADS * DIM // LANES
PER_GROUP = LANES // DIM
FRAMES = 2
ROWS = 8
COLS = 16
TOKENS = ROWS * COLS
CH = HEADS * DIM
OWNERS = 16
HALF = DIM // 2
STATES = 2 * GROUPS
EXTRA = STATES + GROUPS
SLOTS = EXTRA + 1
OWNED = FRAMES * SLOTS
BOTH = 2 * FRAMES * STATES
PIECE = 128
PIECES = FRAMES * TOKENS // PIECE
SPACE = ("row", "col")
VMEM_BYTES = 16 * 1024 * 1024
WIDE_BYTES = 60 * 1024 * 1024
F32 = jnp.float32
BF16 = jnp.bfloat16


def call(body, outs, *args, far=0, unread=0, far_outs=0, scratch=(), flops=1_000_000, vmem=VMEM_BYTES, name=None):
    out_shape = tuple(jax.ShapeDtypeStruct(shape, dtype) for shape, dtype in outs)
    moved = sum(a.size * a.dtype.itemsize for a in args) + sum(o.size * o.dtype.itemsize for o in out_shape)
    near, away = pl.BlockSpec(memory_space=pltpu.VMEM), pl.BlockSpec(memory_space=pltpu.HBM)
    return pl.pallas_call(
        body,
        out_shape=out_shape,
        in_specs=[near] * (len(args) - far - unread) + [away] * far + [pl.BlockSpec(memory_space=pl.ANY)] * unread,
        out_specs=tuple([near] * (len(outs) - far_outs) + [away] * far_outs),
        scratch_shapes=list(scratch),
        compiler_params=pltpu.CompilerParams(vmem_limit_bytes=vmem),
        cost_estimate=pl.CostEstimate(flops=flops, bytes_accessed=moved, transcendentals=0),
        name=name,
    )(*args)


def dot(a, b, contract=((1,), (0,)), precision=None):
    return lax.dot_general(a, b, (contract, ((), ())), preferred_element_type=F32, precision=precision)


def iota(shape, dim):
    return lax.broadcasted_iota(jnp.int32, shape, dim)


def lane_head(shape):
    return iota(shape, 1) // DIM


def compact(square):
    head = lane_head((DIM, LANES))
    out = square[(PER_GROUP - 1) * DIM :]
    for i in reversed(range(PER_GROUP - 1)):
        out = jnp.where(head == i, square[i * DIM : (i + 1) * DIM], out)
    return out


def spread(rows):
    head = lane_head((DIM, LANES))
    return jnp.concatenate([jnp.where(head == i, rows, 0.0) for i in range(PER_GROUP)], axis=0).astype(BF16)


def head_ones():
    return (iota((LANES, LANES), 0) // DIM == lane_head((LANES, LANES))).astype(BF16)


def put_rows(held, size, start, rows):
    for half in range(2):
        held[pl.ds(start + half * GROUPS, OWNERS, stride=size), :] = rows[half * HALF : (half + 1) * HALF]


def take_rows(held, size, start):
    return jnp.concatenate([held[pl.ds(start + half * GROUPS, OWNERS, stride=size), :] for half in range(2)], axis=0)


def part(ref, f, g):
    return ref[f * TOKENS : (f + 1) * TOKENS, g * LANES : (g + 1) * LANES]


def decay_kernel(decay_ref, lanes_ref, row_ref):
    decay = decay_ref[...]
    own = iota((SLOTS, HEADS), 1) // PER_GROUP == iota((SLOTS, HEADS), 0) % GROUPS
    onto = (iota((HEADS, LANES), 0) % PER_GROUP == lane_head((HEADS, LANES))).astype(F32)
    for f in range(FRAMES):
        picked = jnp.where(own, decay[f : f + 1], 0.0)
        lanes_ref[f * SLOTS : (f + 1) * SLOTS, :] = dot(picked, onto, precision=lax.Precision.HIGHEST)
    rest = jnp.broadcast_to(decay[0:1] * decay[1:2], (8, HEADS))
    row = jnp.zeros((8, LANES), F32)
    for third in range(3):
        piece = rest.astype(BF16)
        rest = rest - piece.astype(F32)
        row = row + dot(piece, (iota((HEADS, LANES), 1) == iota((HEADS, LANES), 0) + third * HEADS).astype(BF16))
    row_ref[...] = row


def update_kernel(k_ref, v_ref, out_ref, held, keys, values, sems):
    pieces = [
        [
            pltpu.make_async_copy(source.at[piece], target.at[piece], sems.at[i, j])
            for i, (source, target) in enumerate(((k_ref, keys), (v_ref, values)))
        ]
        for j, piece in enumerate(pl.ds(j * PIECE, PIECE) for j in range(PIECES))
    ]
    for piece in pieces:
        for move in piece:
            move.start()
    for f in range(FRAMES):
        held[pl.ds(f * SLOTS + EXTRA, OWNERS, stride=OWNED), :] = jnp.zeros((OWNERS, LANES), F32)
    for f in range(FRAMES):
        for piece in pieces[f * PIECES // FRAMES : (f + 1) * PIECES // FRAMES]:
            for move in piece:
                move.wait()
        for g in range(GROUPS):
            pos_k = jnp.maximum(part(keys, f, g), 0)
            put_rows(held, OWNED, f * SLOTS + g, compact(dot(pos_k, part(values, f, g), ((0,), (0,)))))
            normal = jnp.sum(pos_k.astype(F32), axis=0, keepdims=True)
            held[pl.ds(f * SLOTS + STATES + g, OWNERS, stride=OWNED), :] = jnp.broadcast_to(normal, (OWNERS, LANES))
    out_ref[...] = held[...].astype(BF16)


def frame_sums(x_ref):
    return jnp.sum(x_ref[...].astype(F32).reshape(OWNERS, OWNED, LANES), axis=0)


def copies(block, out_ref):
    count = out_ref.shape[0] // block.shape[0]
    out_ref[...] = jnp.broadcast_to(block[None], (count,) + block.shape).reshape(out_ref.shape).astype(BF16)


def block_forward_kernel(x_ref, lanes_ref, row_ref, sums_ref, out_ref):
    sums = frame_sums(x_ref)
    sums_ref[...] = sums
    total = lanes_ref[SLOTS:, :] * sums[:SLOTS] + sums[SLOTS:]
    total = jnp.where(iota((SLOTS, LANES), 0) == EXTRA, row_ref[0:1, :], total)
    copies(jnp.concatenate([total, total], axis=0), out_ref)


def shifted(x, by, count):
    row = iota(x.shape, 0)
    if by > 0:
        return jnp.where(row < by, 1.0, pltpu.roll(x, by, 0))
    return jnp.where(row >= count + by, 1.0, pltpu.roll(x, count + by, 0))


def block_weights(held, index, count, backward):
    mine = count - 1 - lax.axis_index("tm")
    decays = held[pl.ds(EXTRA, count, stride=SLOTS), :].astype(BF16)
    source = iota((LANES, LANES), 0)
    onto = (source < 3 * HEADS) & (source % HEADS == index * PER_GROUP + lane_head((LANES, LANES)))
    block = dot(decays, onto.astype(BF16))
    at = iota((count, LANES), 0)
    backward = not backward
    between = at > mine if backward else at < mine
    product = shifted(jnp.where(between, block, 1.0), 1 if backward else -1, count)
    step = 1
    while step < count:
        product = product * shifted(product, step if backward else -step, count)
        step *= 2
    return jnp.where(between, product, 0.0)


def entering(held, carry, weights, count):
    carry[EXTRA:SLOTS, :] = jnp.zeros((1, LANES), F32)
    for slot in range(EXTRA):
        rows = held[pl.ds(slot, count, stride=SLOTS), :]
        carry[slot : slot + 1, :] = jnp.sum(weights[slot % GROUPS] * rows, axis=0, keepdims=True)
    return carry[:SLOTS, :]


def around(x, before, after):
    at = iota(x.shape, 0)
    from_left = jnp.where(at == 0, before, pltpu.roll(x, 1, 0))
    from_right = jnp.where(at == COLS - 1, after, pltpu.roll(x, COLS - 1, 0))
    return from_right, x, from_left


def weighted(taps, row_off, cells):
    tap = (row_off + 1) * 3
    return taps[tap] * cells[0] + taps[tap + 1] * cells[1] + taps[tap + 2] * cells[2]


def from_row(edge, taps, row_off, f):
    corners = edge[FRAMES * COLS :]
    x = edge[f * COLS : (f + 1) * COLS]
    return weighted(taps, row_off, around(x, corners[2 * f : 2 * f + 1], corners[2 * f + 1 : 2 * f + 2]))


def states_kernel(
    y_ref,
    sums_ref,
    lanes_ref,
    q_ref,
    ga_ref,
    pair_ref,
    next_ref,
    weight_ref,
    own_ref,
    inverse_ref,
    num_ref,
    out_ref,
    after_ref,
    held,
    carry,
    sent,
):
    count = y_ref.shape[0] // SLOTS
    held[...] = y_ref[...].astype(F32)
    weights = [block_weights(held, g, count, False) for g in range(GROUPS)]
    before = entering(held, carry, weights, count)
    for g in range(GROUPS):
        after_ref[g] = block_weights(held, g, count, True)
    first = lanes_ref[:SLOTS, :] * before + sums_ref[:SLOTS, :]
    second = lanes_ref[SLOTS:, :] * first + sums_ref[SLOTS:, :]
    own_ref[:SLOTS, :] = first
    own_ref[SLOTS:, :] = second
    for owner in range(OWNERS):
        sent[owner * BOTH : owner * BOTH + STATES, :] = first[:STATES]
        sent[owner * BOTH + STATES : owner * BOTH + 2 * STATES, :] = second[:STATES]
    ones = head_ones()
    for f in range(FRAMES):
        for g in range(GROUPS):
            normal = (first, second)[f][STATES + g : STATES + g + 1]
            pos_q = jnp.maximum(part(q_ref, f, g), 0)
            inverse = 1.0 / (dot((pos_q.astype(F32) * normal).astype(BF16), ones) + 1.0)
            lanes = slice(g * LANES, (g + 1) * LANES)
            taps = [weight_ref[t : t + 1, lanes] for t in range(9)]
            inner = part(ga_ref, f, g)
            above, below = swapped("row", pair_ref[:, lanes].astype(F32), next_ref[:, lanes].astype(F32))
            top = inner[:COLS] + from_row(above, taps, 1, f)
            bottom = inner[-COLS:] + from_row(below, taps, -1, f)
            grad_attn = jnp.concatenate([top, inner[COLS:-COLS], bottom], axis=0)
            grad_num = (grad_attn * inverse).astype(BF16)
            here = (slice(f * TOKENS, (f + 1) * TOKENS), slice(g * LANES, (g + 1) * LANES))
            inverse_ref[here] = inverse
            num_ref[here] = grad_num
            put_rows(sent, BOTH, (FRAMES + f) * STATES + g, compact(dot(pos_q, grad_num, ((0,), (0,)))))
    out_ref[...] = sent[...].astype(BF16)


def locals_kernel(z_ref, q_ref, num_ref, inverse_ref, lanes_ref, sums_ref, den_ref, out_ref, held):
    held[...] = z_ref[...].astype(F32)
    sums = jnp.sum(z_ref[...].astype(F32).reshape(OWNERS, BOTH, LANES), axis=0)
    ones = head_ones()
    lane = iota((TOKENS, LANES), 1) % DIM
    for f in range(FRAMES):
        sums_ref[f * SLOTS : f * SLOTS + STATES, :] = sums[(FRAMES + f) * STATES : (FRAMES + f + 1) * STATES]
        sums_ref[f * SLOTS + EXTRA : (f + 1) * SLOTS, :] = jnp.zeros((1, LANES), F32)
        packed = jnp.zeros((TOKENS, LANES), F32)
        for g in range(GROUPS):
            state = spread(take_rows(held, BOTH, f * STATES + g))
            pos_q = jnp.maximum(part(q_ref, f, g), 0)
            product = part(num_ref, f, g).astype(F32) * dot(pos_q, state)
            grad_den = -dot(product.astype(BF16), ones) * part(inverse_ref, f, g)
            packed = packed + jnp.where(lane == g, grad_den, 0.0)
            at = f * SLOTS + STATES + g
            sums_ref[at : at + 1, :] = jnp.sum(grad_den * pos_q.astype(F32), axis=0, keepdims=True)
        den_ref[f * TOKENS : (f + 1) * TOKENS, :] = packed.astype(BF16)
    total = lanes_ref[:SLOTS, :] * (sums_ref[:SLOTS, :] + lanes_ref[SLOTS:, :] * sums_ref[SLOTS:, :])
    copies(jnp.concatenate([total, total], axis=0), out_ref)


def query_kernel(z_ref, q_ref, num_ref, den_ref, own_ref, grad_ref, held):
    held[...] = z_ref[...].astype(F32)
    source = iota((LANES, LANES), 0)
    same = source // DIM == lane_head((LANES, LANES))
    for f in range(FRAMES):
        den = den_ref[f * TOKENS : (f + 1) * TOKENS, :]
        for g in range(GROUPS):
            state = spread(take_rows(held, BOTH, f * STATES + g))
            at = f * SLOTS + STATES + g
            here = (slice(f * TOKENS, (f + 1) * TOKENS), slice(g * LANES, (g + 1) * LANES))
            grad_den = dot(den, (same & (source % DIM == g)).astype(BF16))
            grad = dot(num_ref[here], state, ((1,), (1,))) + grad_den * own_ref[at : at + 1, :]
            grad_ref[here] = jnp.where(q_ref[here].astype(F32) > 0, grad, 0.0).astype(BF16)


def carried_kernel(y_ref, sums_ref, lanes_ref, weights_ref, out_ref, held, carry):
    count = y_ref.shape[0] // SLOTS
    held[...] = y_ref[...].astype(F32)
    after = entering(held, carry, [weights_ref[g] for g in range(GROUPS)], count)
    second = sums_ref[SLOTS:, :] + after
    first = sums_ref[:SLOTS, :] + lanes_ref[SLOTS:, :] * second
    copies(jnp.concatenate([first, second], axis=0), out_ref)


def swapped(axis, first, second):
    odd = lax.axis_index(axis) % 2 == 1
    return jnp.where(odd, first, second), jnp.where(odd, second, first)


def edge_cols_kernel(g_ref, inner_ref, outer_ref, first, last):
    for at in range(FRAMES * ROWS):
        x = g_ref[at * COLS : (at + 1) * COLS, :].astype(F32)
        first[at : at + 1, :] = x[:1]
        last[at : at + 1, :] = x[COLS - 1 :]
    inner, outer = swapped("col", first[...], last[...])
    inner_ref[...] = inner.astype(BF16)
    outer_ref[...] = outer.astype(BF16)


def edge_rows_kernel(g_ref, pair_ref, next_ref, inner_ref, outer_ref, corners):
    left, right = swapped("col", pair_ref[...].astype(F32), next_ref[...].astype(F32))
    edges = []
    for row in (0, ROWS - 1):
        corners[...] = jnp.zeros(corners.shape, F32)
        cells = []
        for f in range(FRAMES):
            at = f * ROWS + row
            cells.append(g_ref[at * COLS : (at + 1) * COLS, :].astype(F32))
            corners[2 * f : 2 * f + 1, :] = left[at : at + 1]
            corners[2 * f + 1 : 2 * f + 2, :] = right[at : at + 1]
        edges.append(jnp.concatenate(cells + [corners[...]], axis=0))
    inner, outer = swapped("row", *edges)
    inner_ref[...] = inner.astype(BF16)
    outer_ref[...] = outer.astype(BF16)


def conv_kernel(g_ref, pair_ref, next_ref, weight_ref, out_ref):
    left, right = swapped("col", pair_ref[...].astype(F32), next_ref[...].astype(F32))
    for f in range(FRAMES):
        for g in range(GROUPS):
            lanes = slice(g * LANES, (g + 1) * LANES)
            taps = [weight_ref[t : t + 1, lanes] for t in range(9)]
            total = [None] * ROWS
            for source in range(ROWS):
                first = f * ROWS + source
                x = g_ref[first * COLS : (first + 1) * COLS, lanes].astype(F32)
                cells = around(x, left[first : first + 1, lanes], right[first : first + 1, lanes])
                for row_off in (-1, 0, 1):
                    row = source + row_off
                    if 0 <= row < ROWS:
                        add = weighted(taps, row_off, cells)
                        if row_off == 0:
                            add = add + x
                        total[row] = add if total[row] is None else total[row] + add
            for row in range(ROWS):
                first = (f * ROWS + row) * COLS
                out_ref[first : first + COLS, lanes] = total[row]


def key_kernel(k_ref, v_ref, z_ref, key_grad_ref, value_grad_ref, held, key_grad, value_grad, sems):
    held[...] = z_ref[...].astype(F32)
    sums = frame_sums(z_ref)
    moves = []
    for f in range(FRAMES):
        for g in range(GROUPS):
            carried = spread(take_rows(held, OWNED, f * SLOTS + g))
            at = f * SLOTS + STATES + g
            keys = part(k_ref, f, g)
            here = (slice(f * TOKENS, (f + 1) * TOKENS), slice(g * LANES, (g + 1) * LANES))
            grad = dot(part(v_ref, f, g), carried, ((1,), (1,))) + sums[at : at + 1]
            key_grad[here] = jnp.where(keys.astype(F32) > 0, grad, 0.0).astype(BF16)
            value_grad[here] = dot(jnp.maximum(keys, 0), carried).astype(BF16)
        for j in range(f * PIECES // FRAMES, (f + 1) * PIECES // FRAMES):
            piece = pl.ds(j * PIECE, PIECE)
            for i, (source, target) in enumerate(((key_grad, key_grad_ref), (value_grad, value_grad_ref))):
                move = pltpu.make_async_copy(source.at[piece], target.at[piece], sems.at[i, j])
                move.start()
                moves.append(move)
    for move in moves:
        move.wait()


def exchange(block, axes, count):
    rows = block.shape[0] // count
    block = block.reshape(count, rows // 2, 2, LANES)
    groups = [list(reversed(range(count)))]
    return lax.all_to_all(block, axes, 0, 0, tiled=True, axis_index_groups=groups).reshape(count * rows, LANES)


def neighbours(inner, outer, axis):
    count = lax.axis_size(axis)
    pairs = [[(i, i + 1) for i in range(start, count - 1, 2)] for start in range(2)]
    return tuple(
        lax.ppermute(edge, axis, [way for a, b in pair for way in ((a, b), (b, a))])
        for edge, pair in zip((inner, outer), pairs)
    )


def per_device(query_tokens, key_tokens, value_tokens, grad_output, frame_decay, conv_weight):
    shape = query_tokens.shape
    flat = (FRAMES * TOKENS, CH)
    blocks = lax.axis_size("tm")
    q, k, v, g = (x.reshape(flat) for x in (query_tokens, key_tokens, value_tokens, grad_output))
    space = ((OWNERS * OWNED, LANES), BF16)
    both = ((OWNERS * BOTH, LANES), BF16)
    time = ((blocks * SLOTS, LANES), BF16)
    owned = ((OWNED, LANES), F32)
    held_space, held_both, held_time = (pltpu.VMEM(kind[0], F32) for kind in (space, both, time))
    carry = pltpu.VMEM((32, LANES), F32)
    work = 2 * FRAMES * GROUPS * TOKENS * LANES * LANES

    buffer = pltpu.VMEM(flat, BF16)
    copies_done = pltpu.SemaphoreType.DMA((2, PIECES))
    (sent,) = call(
        update_kernel,
        [space],
        k,
        v,
        far=2,
        scratch=[held_space, buffer, buffer, copies_done],
        flops=work,
        vmem=WIDE_BYTES,
        name="update",
    )
    lanes, decay_row = call(decay_kernel, [owned, ((8, LANES), F32)], frame_decay, name="decay")
    x = exchange(sent, SPACE, OWNERS)
    side = ((FRAMES * ROWS, CH), BF16)
    edge = ((FRAMES * COLS + 16, CH), BF16)
    held_side = pltpu.VMEM(side[0], F32)
    inner, outer = call(edge_cols_kernel, [side, side], g, scratch=[held_side, held_side], name="edge_cols")
    beside = neighbours(inner, outer, "col")
    inner, outer = call(
        edge_rows_kernel, [edge, edge], g, *beside, scratch=[held_side], flops=20_000_000_000, name="edge_rows"
    )
    across = neighbours(inner, outer, "row")
    sums, sent = call(block_forward_kernel, [owned, time], x, lanes, decay_row, name="block_forward")
    y = exchange(sent, "tm", blocks)
    (grad_attn,) = call(
        conv_kernel, [(flat, F32)], g, *beside, conv_weight, flops=20 * flat[0] * flat[1], name="conv"
    )
    own, inverse, grad_num, sent, weights = call(
        states_kernel,
        [owned, (flat, F32), (flat, BF16), both, ((GROUPS, blocks, LANES), F32)],
        y,
        sums,
        lanes,
        q,
        grad_attn,
        *across,
        conv_weight,
        scratch=[held_time, carry, held_both],
        flops=2 * work,
        name="states",
    )
    z = exchange(sent, SPACE, OWNERS)
    sums, grad_den, sent = call(
        locals_kernel,
        [owned, ((FRAMES * TOKENS, LANES), BF16), time],
        z,
        q,
        grad_num,
        inverse,
        lanes,
        scratch=[held_both],
        flops=2 * work,
        name="locals",
    )
    y = exchange(sent, "tm", blocks)
    (query_grad,) = call(
        query_kernel, [(flat, BF16)], z, q, grad_num, grad_den, own, scratch=[held_both], flops=work, name="query"
    )
    (sent,) = call(carried_kernel, [space], y, sums, lanes, weights, scratch=[held_time, carry], name="carried")
    z = exchange(sent, SPACE, OWNERS)
    key_grad, value_grad = call(
        key_kernel,
        [(flat, BF16), (flat, BF16)],
        k,
        v,
        z,
        far_outs=2,
        scratch=[held_space, buffer, buffer, copies_done],
        flops=2 * work,
        name="key",
    )
    return query_grad.reshape(shape), key_grad.reshape(shape), value_grad.reshape(shape)


def solution(mesh):
    tokens = P("tm", "row", "col", None)
    return jax.shard_map(
        per_device,
        mesh=mesh,
        in_specs=(tokens, tokens, tokens, tokens, P("tm", None), P()),
        out_specs=(tokens, tokens, tokens),
        check_vma=False,
    )
```

```python
import jax
import jax.numpy as jnp
from jax import lax
from jax.experimental import pallas as pl
from jax.experimental.pallas import tpu as pltpu
from jax.sharding import PartitionSpec as P

HEADS = 36
DIM = 32
LANES = 128
GROUPS = HEADS * DIM // LANES
PER_GROUP = LANES // DIM
FRAMES = 2
ROWS = 8
COLS = 16
TOKENS = ROWS * COLS
CH = HEADS * DIM
OWNERS = 16
HALF = DIM // 2
STATES = 2 * GROUPS
EXTRA = STATES + GROUPS
SLOTS = EXTRA + 1
OWNED = FRAMES * SLOTS
BOTH = 2 * FRAMES * STATES
PIECE = 128
PIECES = FRAMES * TOKENS // PIECE
SPACE = ("row", "col")
VMEM_BYTES = 16 * 1024 * 1024
WIDE_BYTES = 60 * 1024 * 1024
F32 = jnp.float32
BF16 = jnp.bfloat16


def call(body, outs, *args, far=0, unread=0, far_outs=0, scratch=(), flops=1_000_000, vmem=VMEM_BYTES, name=None):
    out_shape = tuple(jax.ShapeDtypeStruct(shape, dtype) for shape, dtype in outs)
    moved = sum(a.size * a.dtype.itemsize for a in args) + sum(o.size * o.dtype.itemsize for o in out_shape)
    near, away = pl.BlockSpec(memory_space=pltpu.VMEM), pl.BlockSpec(memory_space=pltpu.HBM)
    return pl.pallas_call(
        body,
        out_shape=out_shape,
        in_specs=[near] * (len(args) - far - unread) + [away] * far + [pl.BlockSpec(memory_space=pl.ANY)] * unread,
        out_specs=tuple([near] * (len(outs) - far_outs) + [away] * far_outs),
        scratch_shapes=list(scratch),
        compiler_params=pltpu.CompilerParams(vmem_limit_bytes=vmem),
        cost_estimate=pl.CostEstimate(flops=flops, bytes_accessed=moved, transcendentals=0),
        name=name,
    )(*args)


def dot(a, b, contract=((1,), (0,)), precision=None):
    return lax.dot_general(a, b, (contract, ((), ())), preferred_element_type=F32, precision=precision)


def iota(shape, dim):
    return lax.broadcasted_iota(jnp.int32, shape, dim)


def lane_head(shape):
    return iota(shape, 1) // DIM


def compact(square):
    head = lane_head((DIM, LANES))
    out = square[(PER_GROUP - 1) * DIM :]
    for i in reversed(range(PER_GROUP - 1)):
        out = jnp.where(head == i, square[i * DIM : (i + 1) * DIM], out)
    return out


def spread(rows):
    head = lane_head((DIM, LANES))
    return jnp.concatenate([jnp.where(head == i, rows, 0.0) for i in range(PER_GROUP)], axis=0).astype(BF16)


def head_ones():
    return (iota((LANES, LANES), 0) // DIM == lane_head((LANES, LANES))).astype(BF16)


def put_rows(held, size, start, rows):
    for half in range(2):
        held[pl.ds(start + half * GROUPS, OWNERS, stride=size), :] = rows[half * HALF : (half + 1) * HALF]


def take_rows(held, size, start):
    return jnp.concatenate([held[pl.ds(start + half * GROUPS, OWNERS, stride=size), :] for half in range(2)], axis=0)


def part(ref, f, g):
    return ref[f * TOKENS : (f + 1) * TOKENS, g * LANES : (g + 1) * LANES]


def decay_kernel(decay_ref, lanes_ref, row_ref):
    decay = decay_ref[...]
    own = iota((SLOTS, HEADS), 1) // PER_GROUP == iota((SLOTS, HEADS), 0) % GROUPS
    onto = (iota((HEADS, LANES), 0) % PER_GROUP == lane_head((HEADS, LANES))).astype(F32)
    for f in range(FRAMES):
        picked = jnp.where(own, decay[f : f + 1], 0.0)
        lanes_ref[f * SLOTS : (f + 1) * SLOTS, :] = dot(picked, onto, precision=lax.Precision.HIGHEST)
    rest = jnp.broadcast_to(decay[0:1] * decay[1:2], (8, HEADS))
    row = jnp.zeros((8, LANES), F32)
    for third in range(3):
        piece = rest.astype(BF16)
        rest = rest - piece.astype(F32)
        row = row + dot(piece, (iota((HEADS, LANES), 1) == iota((HEADS, LANES), 0) + third * HEADS).astype(BF16))
    row_ref[...] = row


def update_kernel(k_ref, v_ref, out_ref, held, keys, values, sems):
    pieces = [
        [
            pltpu.make_async_copy(source.at[piece], target.at[piece], sems.at[i, j])
            for i, (source, target) in enumerate(((k_ref, keys), (v_ref, values)))
        ]
        for j, piece in enumerate(pl.ds(j * PIECE, PIECE) for j in range(PIECES))
    ]
    for piece in pieces:
        for move in piece:
            move.start()
    for f in range(FRAMES):
        held[pl.ds(f * SLOTS + EXTRA, OWNERS, stride=OWNED), :] = jnp.zeros((OWNERS, LANES), F32)
    for f in range(FRAMES):
        for piece in pieces[f * PIECES // FRAMES : (f + 1) * PIECES // FRAMES]:
            for move in piece:
                move.wait()
        for g in range(GROUPS):
            pos_k = jnp.maximum(part(keys, f, g), 0)
            put_rows(held, OWNED, f * SLOTS + g, compact(dot(pos_k, part(values, f, g), ((0,), (0,)))))
            normal = jnp.sum(pos_k.astype(F32), axis=0, keepdims=True)
            held[pl.ds(f * SLOTS + STATES + g, OWNERS, stride=OWNED), :] = jnp.broadcast_to(normal, (OWNERS, LANES))
    out_ref[...] = held[...].astype(BF16)


def frame_sums(x_ref):
    return jnp.sum(x_ref[...].astype(F32).reshape(OWNERS, OWNED, LANES), axis=0)


def copies(block, out_ref):
    count = out_ref.shape[0] // block.shape[0]
    out_ref[...] = jnp.broadcast_to(block[None], (count,) + block.shape).reshape(out_ref.shape).astype(BF16)


def block_forward_kernel(x_ref, lanes_ref, row_ref, sums_ref, out_ref):
    sums = frame_sums(x_ref)
    sums_ref[...] = sums
    total = lanes_ref[SLOTS:, :] * sums[:SLOTS] + sums[SLOTS:]
    total = jnp.where(iota((SLOTS, LANES), 0) == EXTRA, row_ref[0:1, :], total)
    copies(jnp.concatenate([total, total], axis=0), out_ref)


def shifted(x, by, count):
    row = iota(x.shape, 0)
    if by > 0:
        return jnp.where(row < by, 1.0, pltpu.roll(x, by, 0))
    return jnp.where(row >= count + by, 1.0, pltpu.roll(x, count + by, 0))


def block_weights(held, index, count, backward):
    mine = count - 1 - lax.axis_index("tm")
    decays = held[pl.ds(EXTRA, count, stride=SLOTS), :].astype(BF16)
    source = iota((LANES, LANES), 0)
    onto = (source < 3 * HEADS) & (source % HEADS == index * PER_GROUP + lane_head((LANES, LANES)))
    block = dot(decays, onto.astype(BF16))
    at = iota((count, LANES), 0)
    backward = not backward
    between = at > mine if backward else at < mine
    product = shifted(jnp.where(between, block, 1.0), 1 if backward else -1, count)
    step = 1
    while step < count:
        product = product * shifted(product, step if backward else -step, count)
        step *= 2
    return jnp.where(between, product, 0.0)


def entering(held, carry, weights, count):
    carry[EXTRA:SLOTS, :] = jnp.zeros((1, LANES), F32)
    for slot in range(EXTRA):
        rows = held[pl.ds(slot, count, stride=SLOTS), :]
        carry[slot : slot + 1, :] = jnp.sum(weights[slot % GROUPS] * rows, axis=0, keepdims=True)
    return carry[:SLOTS, :]


def around(x, before, after):
    at = iota(x.shape, 0)
    from_left = jnp.where(at == 0, before, pltpu.roll(x, 1, 0))
    from_right = jnp.where(at == COLS - 1, after, pltpu.roll(x, COLS - 1, 0))
    return from_right, x, from_left


def weighted(taps, row_off, cells):
    tap = (row_off + 1) * 3
    return taps[tap] * cells[0] + taps[tap + 1] * cells[1] + taps[tap + 2] * cells[2]


def from_row(edge, taps, row_off, f):
    corners = edge[FRAMES * COLS :]
    x = edge[f * COLS : (f + 1) * COLS]
    return weighted(taps, row_off, around(x, corners[2 * f : 2 * f + 1], corners[2 * f + 1 : 2 * f + 2]))


def states_kernel(
    y_ref,
    sums_ref,
    lanes_ref,
    q_ref,
    ga_ref,
    next_ref,
    pair_ref,
    weight_ref,
    own_ref,
    inverse_ref,
    num_ref,
    out_ref,
    after_ref,
    held,
    carry,
    sent,
):
    count = y_ref.shape[0] // SLOTS
    held[...] = y_ref[...].astype(F32)
    weights = [block_weights(held, g, count, False) for g in range(GROUPS)]
    before = entering(held, carry, weights, count)
    for g in range(GROUPS):
        after_ref[g] = block_weights(held, g, count, True)
    first = lanes_ref[:SLOTS, :] * before + sums_ref[:SLOTS, :]
    second = lanes_ref[SLOTS:, :] * first + sums_ref[SLOTS:, :]
    own_ref[:SLOTS, :] = first
    own_ref[SLOTS:, :] = second
    for owner in range(OWNERS):
        sent[owner * BOTH : owner * BOTH + STATES, :] = first[:STATES]
        sent[owner * BOTH + STATES : owner * BOTH + 2 * STATES, :] = second[:STATES]
    ones = head_ones()
    for f in range(FRAMES):
        for g in range(GROUPS):
            normal = (first, second)[f][STATES + g : STATES + g + 1]
            pos_q = jnp.maximum(part(q_ref, f, g), 0)
            inverse = 1.0 / (dot((pos_q.astype(F32) * normal).astype(BF16), ones) + 1.0)
            lanes = slice(g * LANES, (g + 1) * LANES)
            taps = [weight_ref[t : t + 1, lanes] for t in range(9)]
            inner = part(ga_ref, f, g)
            above, below = swapped("row", pair_ref[:, lanes].astype(F32), next_ref[:, lanes].astype(F32))
            top = inner[:COLS] + from_row(above, taps, 1, f)
            bottom = inner[-COLS:] + from_row(below, taps, -1, f)
            grad_attn = jnp.concatenate([top, inner[COLS:-COLS], bottom], axis=0)
            grad_num = (grad_attn * inverse).astype(BF16)
            here = (slice(f * TOKENS, (f + 1) * TOKENS), slice(g * LANES, (g + 1) * LANES))
            inverse_ref[here] = inverse
            num_ref[here] = grad_num
            put_rows(sent, BOTH, (FRAMES + f) * STATES + g, compact(dot(pos_q, grad_num, ((0,), (0,)))))
    out_ref[...] = sent[...].astype(BF16)


def locals_kernel(z_ref, q_ref, num_ref, inverse_ref, lanes_ref, sums_ref, den_ref, out_ref, held):
    held[...] = z_ref[...].astype(F32)
    sums = jnp.sum(z_ref[...].astype(F32).reshape(OWNERS, BOTH, LANES), axis=0)
    ones = head_ones()
    lane = iota((TOKENS, LANES), 1) % DIM
    for f in range(FRAMES):
        sums_ref[f * SLOTS : f * SLOTS + STATES, :] = sums[(FRAMES + f) * STATES : (FRAMES + f + 1) * STATES]
        sums_ref[f * SLOTS + EXTRA : (f + 1) * SLOTS, :] = jnp.zeros((1, LANES), F32)
        packed = jnp.zeros((TOKENS, LANES), F32)
        for g in range(GROUPS):
            state = spread(take_rows(held, BOTH, f * STATES + g))
            pos_q = jnp.maximum(part(q_ref, f, g), 0)
            product = part(num_ref, f, g).astype(F32) * dot(pos_q, state)
            grad_den = -dot(product.astype(BF16), ones) * part(inverse_ref, f, g)
            packed = packed + jnp.where(lane == g, grad_den, 0.0)
            at = f * SLOTS + STATES + g
            sums_ref[at : at + 1, :] = jnp.sum(grad_den * pos_q.astype(F32), axis=0, keepdims=True)
        den_ref[f * TOKENS : (f + 1) * TOKENS, :] = packed.astype(BF16)
    total = lanes_ref[:SLOTS, :] * (sums_ref[:SLOTS, :] + lanes_ref[SLOTS:, :] * sums_ref[SLOTS:, :])
    copies(jnp.concatenate([total, total], axis=0), out_ref)


def query_kernel(z_ref, q_ref, num_ref, den_ref, own_ref, grad_ref, held):
    held[...] = z_ref[...].astype(F32)
    source = iota((LANES, LANES), 0)
    same = source // DIM == lane_head((LANES, LANES))
    for f in range(FRAMES):
        den = den_ref[f * TOKENS : (f + 1) * TOKENS, :]
        for g in range(GROUPS):
            state = spread(take_rows(held, BOTH, f * STATES + g))
            at = f * SLOTS + STATES + g
            here = (slice(f * TOKENS, (f + 1) * TOKENS), slice(g * LANES, (g + 1) * LANES))
            grad_den = dot(den, (same & (source % DIM == g)).astype(BF16))
            grad = dot(num_ref[here], state, ((1,), (1,))) + grad_den * own_ref[at : at + 1, :]
            grad_ref[here] = jnp.where(q_ref[here].astype(F32) > 0, grad, 0.0).astype(BF16)


def carried_kernel(y_ref, sums_ref, lanes_ref, weights_ref, out_ref, held, carry):
    count = y_ref.shape[0] // SLOTS
    held[...] = y_ref[...].astype(F32)
    after = entering(held, carry, [weights_ref[g] for g in range(GROUPS)], count)
    second = sums_ref[SLOTS:, :] + after
    first = sums_ref[:SLOTS, :] + lanes_ref[SLOTS:, :] * second
    copies(jnp.concatenate([first, second], axis=0), out_ref)


def swapped(axis, first, second):
    odd = lax.axis_index(axis) % 2 == 1
    return jnp.where(odd, first, second), jnp.where(odd, second, first)


def edge_cols_kernel(g_ref, inner_ref, outer_ref, first, last):
    for at in range(FRAMES * ROWS):
        x = g_ref[at * COLS : (at + 1) * COLS, :].astype(F32)
        first[at : at + 1, :] = x[:1]
        last[at : at + 1, :] = x[COLS - 1 :]
    inner, outer = swapped("col", first[...], last[...])
    inner_ref[...] = inner.astype(BF16)
    outer_ref[...] = outer.astype(BF16)


def edge_rows_kernel(g_ref, pair_ref, next_ref, outer_ref, inner_ref, corners):
    left, right = swapped("col", pair_ref[...].astype(F32), next_ref[...].astype(F32))
    edges = []
    for row in (0, ROWS - 1):
        corners[...] = jnp.zeros(corners.shape, F32)
        cells = []
        for f in range(FRAMES):
            at = f * ROWS + row
            cells.append(g_ref[at * COLS : (at + 1) * COLS, :].astype(F32))
            corners[2 * f : 2 * f + 1, :] = left[at : at + 1]
            corners[2 * f + 1 : 2 * f + 2, :] = right[at : at + 1]
        edges.append(jnp.concatenate(cells + [corners[...]], axis=0))
    inner, outer = swapped("row", *edges)
    inner_ref[...] = inner.astype(BF16)
    outer_ref[...] = outer.astype(BF16)


def conv_kernel(g_ref, pair_ref, next_ref, weight_ref, out_ref):
    left, right = swapped("col", pair_ref[...].astype(F32), next_ref[...].astype(F32))
    for f in range(FRAMES):
        for g in range(GROUPS):
            lanes = slice(g * LANES, (g + 1) * LANES)
            taps = [weight_ref[t : t + 1, lanes] for t in range(9)]
            total = [None] * ROWS
            for source in range(ROWS):
                first = f * ROWS + source
                x = g_ref[first * COLS : (first + 1) * COLS, lanes].astype(F32)
                cells = around(x, left[first : first + 1, lanes], right[first : first + 1, lanes])
                for row_off in (-1, 0, 1):
                    row = source + row_off
                    if 0 <= row < ROWS:
                        add = weighted(taps, row_off, cells)
                        if row_off == 0:
                            add = add + x
                        total[row] = add if total[row] is None else total[row] + add
            for row in range(ROWS):
                first = (f * ROWS + row) * COLS
                out_ref[first : first + COLS, lanes] = total[row]


def key_kernel(k_ref, v_ref, z_ref, key_grad_ref, value_grad_ref, held, key_grad, value_grad, sems):
    held[...] = z_ref[...].astype(F32)
    sums = frame_sums(z_ref)
    moves = []
    for f in range(FRAMES):
        for g in range(GROUPS):
            carried = spread(take_rows(held, OWNED, f * SLOTS + g))
            at = f * SLOTS + STATES + g
            keys = part(k_ref, f, g)
            here = (slice(f * TOKENS, (f + 1) * TOKENS), slice(g * LANES, (g + 1) * LANES))
            grad = dot(part(v_ref, f, g), carried, ((1,), (1,))) + sums[at : at + 1]
            key_grad[here] = jnp.where(keys.astype(F32) > 0, grad, 0.0).astype(BF16)
            value_grad[here] = dot(jnp.maximum(keys, 0), carried).astype(BF16)
        for j in range(f * PIECES // FRAMES, (f + 1) * PIECES // FRAMES):
            piece = pl.ds(j * PIECE, PIECE)
            for i, (source, target) in enumerate(((key_grad, key_grad_ref), (value_grad, value_grad_ref))):
                move = pltpu.make_async_copy(source.at[piece], target.at[piece], sems.at[i, j])
                move.start()
                moves.append(move)
    for move in moves:
        move.wait()


def exchange(block, axes, count):
    rows = block.shape[0] // count
    block = block.reshape(count, rows // 2, 2, LANES)
    groups = [list(reversed(range(count)))]
    return lax.all_to_all(block, axes, 0, 0, tiled=True, axis_index_groups=groups).reshape(count * rows, LANES)


def neighbours(inner, outer, axis):
    count = lax.axis_size(axis)
    pairs = [[(i, i + 1) for i in range(start, count - 1, 2)] for start in range(2)]
    far, near = (
        lax.ppermute(edge, axis, [way for a, b in pair for way in ((a, b), (b, a))])
        for edge, pair in zip((outer, inner), reversed(pairs))
    )
    return near, far


def per_device(query_tokens, key_tokens, value_tokens, grad_output, frame_decay, conv_weight):
    shape = query_tokens.shape
    flat = (FRAMES * TOKENS, CH)
    blocks = lax.axis_size("tm")
    q, k, v, g = (x.reshape(flat) for x in (query_tokens, key_tokens, value_tokens, grad_output))
    space = ((OWNERS * OWNED, LANES), BF16)
    both = ((OWNERS * BOTH, LANES), BF16)
    time = ((blocks * SLOTS, LANES), BF16)
    owned = ((OWNED, LANES), F32)
    held_space, held_both, held_time = (pltpu.VMEM(kind[0], F32) for kind in (space, both, time))
    carry = pltpu.VMEM((32, LANES), F32)
    work = 2 * FRAMES * GROUPS * TOKENS * LANES * LANES

    buffer = pltpu.VMEM(flat, BF16)
    copies_done = pltpu.SemaphoreType.DMA((2, PIECES))
    (sent,) = call(
        update_kernel,
        [space],
        k,
        v,
        far=2,
        scratch=[held_space, buffer, buffer, copies_done],
        flops=work,
        vmem=WIDE_BYTES,
        name="update",
    )
    lanes, decay_row = call(decay_kernel, [owned, ((8, LANES), F32)], frame_decay, name="decay")
    x = exchange(sent, SPACE, OWNERS)
    side = ((FRAMES * ROWS, CH), BF16)
    edge = ((FRAMES * COLS + 16, CH), BF16)
    held_side = pltpu.VMEM(side[0], F32)
    inner, outer = call(edge_cols_kernel, [side, side], g, scratch=[held_side, held_side], name="edge_cols")
    beside = neighbours(inner, outer, "col")
    outer, inner = call(
        edge_rows_kernel, [edge, edge], g, *beside, scratch=[held_side], flops=20_000_000_000, name="edge_rows"
    )
    across = neighbours(inner, outer, "row")
    sums, sent = call(block_forward_kernel, [owned, time], x, lanes, decay_row, name="block_forward")
    y = exchange(sent, "tm", blocks)
    (grad_attn,) = call(
        conv_kernel, [(flat, F32)], g, *beside, conv_weight, flops=20 * flat[0] * flat[1], name="conv"
    )
    own, inverse, grad_num, sent, weights = call(
        states_kernel,
        [owned, (flat, F32), (flat, BF16), both, ((GROUPS, blocks, LANES), F32)],
        y,
        sums,
        lanes,
        q,
        grad_attn,
        *reversed(across),
        conv_weight,
        scratch=[held_time, carry, held_both],
        flops=2 * work,
        name="states",
    )
    z = exchange(sent, SPACE, OWNERS)
    sums, grad_den, sent = call(
        locals_kernel,
        [owned, ((FRAMES * TOKENS, LANES), BF16), time],
        z,
        q,
        grad_num,
        inverse,
        lanes,
        scratch=[held_both],
        flops=2 * work,
        name="locals",
    )
    y = exchange(sent, "tm", blocks)
    (query_grad,) = call(
        query_kernel, [(flat, BF16)], z, q, grad_num, grad_den, own, scratch=[held_both], flops=work, name="query"
    )
    (sent,) = call(carried_kernel, [space], y, sums, lanes, weights, scratch=[held_time, carry], name="carried")
    z = exchange(sent, SPACE, OWNERS)
    key_grad, value_grad = call(
        key_kernel,
        [(flat, BF16), (flat, BF16)],
        k,
        v,
        z,
        far_outs=2,
        scratch=[held_space, buffer, buffer, copies_done],
        flops=2 * work,
        name="key",
    )
    return query_grad.reshape(shape), key_grad.reshape(shape), value_grad.reshape(shape)


def solution(mesh):
    tokens = P("tm", "row", "col", None)
    return jax.shard_map(
        per_device,
        mesh=mesh,
        in_specs=(tokens, tokens, tokens, tokens, P("tm", None), P()),
        out_specs=(tokens, tokens, tokens),
        check_vma=False,
    )
```
